128 devices in a mesh: ctx: 32 (over x_hi, z, y), ep: 4 (over x_lo, core).
Axes of the slice: x: 4 (x_hi: 2, x_lo: 2; x = x_hi * 2 + x_lo), y: 4, z: 4, core: 2. Of those that a mesh axis runs over, the one named last changes fastest.
Arguments:
- q_nope: bfloat16 [4096, 8192], P('ctx', 'ep'), may hold values from -6 to 6
- q_rope: bfloat16 [4096, 4096], P('ctx', 'ep'), may hold values from -300 to 300
- latent: bfloat16 [4096, 512], P('ctx'), may hold values from -6 to 6
- k_rope: bfloat16 [4096, 64], P('ctx'), may hold values from -5 to 5
- w_uk: bfloat16 [512, 8192], P(None, 'ep'), may hold values from -0.25 to 0.25
- w_uv: bfloat16 [512, 8192], P(None, 'ep'), may hold values from -0.25 to 0.25
- positions: int32 [4096], replicated, may hold values from 0 to 4095, as said below
- moe_rows: bfloat16 [4096, 7168], P('ctx', 'ep'), may hold values from -6 to 6
- expert_ids: int32 [4096, 8], P('ctx'), may hold values from 0 to 255, all different within a row; in each aligned block of 128 rows (0 to 127, 128 to 255, ...) at most 8 rows name the same one
- expert_weights: float32 [4096, 8], P('ctx'), may hold values from 0.05 to 0.5
- w_gate: bfloat16 [32, 7168, 1024], P('ctx', None, 'ep'), may hold values from -0.0625 to 0.0625
- w_up: bfloat16 [32, 7168, 1024], P('ctx', None, 'ep'), may hold values from -0.0625 to 0.0625
- w_down: bfloat16 [32, 1024, 7168], P('ctx', 'ep'), may hold values from -0.1875 to 0.1875
Outputs:
- attention: bfloat16 [4096, 8192], P('ctx', 'ep')
- moe_out: bfloat16 [4096, 7168], P('ctx', 'ep')
The draws below stay inside these ranges and needn't reach their ends.
Inputs may be any that keep to these rules, and one draw needn't show every extreme that they name: `expert_ids`: each row names 8 different experts; in each aligned block of 128 rows (the rows of one index of ctx) no expert is named by more than 8 rows. A permutation of the positions; the 128 rows of each index of ctx are two runs of 64 consecutive positions, run j and run 2 * 32 - 1 - j of the prompt for some j.
All inputs are finite; a program needn't handle non-finite values.
Results may differ from the reference program's by a relative error of at most 0.017.
Values may be sent and summed in bfloat16 or wider, within the bound.
A program may use at most 192 MiB of HBM per device.

```python
import math
import jax
import jax.numpy as jnp
import numpy as np
from jax import lax

D = 7168
F = 1024
HEADS = 64
NOPE = 128
ROPE = 64
VDIM = 128
LAT = 512
EXPERTS = 256
TOP = 8
TQ = 128
ROWS = 128
HALF = 64
SEQ = 4096
MOE_TOKENS = 4096
EXP_WIN = 32
CAP = 8
N_CTX = 32


def rope_pair(key):
    key_base = jax.random.fold_in(key, 0)
    key_query = jax.random.fold_in(key, 4)
    keys_rope = jnp.clip(jax.random.normal(key_base, (SEQ, ROPE), jnp.float32), -4.0, 4.0)
    keys_out = keys_rope
    queries = jnp.clip(jax.random.normal(key_query, (SEQ, HEADS, ROPE), jnp.float32), -6.0, 6.0)
    return (keys_out, queries.reshape(SEQ, HEADS * ROPE))


def draw_q_rope(key, part):
    keys_out, queries = rope_pair(key)
    return queries.astype(jnp.bfloat16)


def draw_k_rope(key, part):
    keys_out, queries = rope_pair(key)
    return keys_out.astype(jnp.bfloat16)


def draw_positions(key, part):
    key = jax.random.fold_in(key, 7)
    block_count = SEQ // TQ
    order = jax.random.permutation(key, block_count).astype(jnp.int32)
    lanes = jnp.arange(HALF, dtype=jnp.int32)
    first_run = order[:, None] * HALF + lanes[None, :]
    second_run = (2 * block_count - 1 - order)[:, None] * HALF + lanes[None, :]
    return jnp.concatenate([first_run, second_run], axis=1).reshape(SEQ).astype(jnp.int32)


def block_scale(stream_key, extent, pieces, least, largest):
    loudness, own = 1.0, jax.random.fold_in(stream_key, 6)
    for position, shards_of in pieces:
        steps = jnp.exp(jax.random.uniform(jax.random.fold_in(own, position), (shards_of,), jnp.float32, least / len(pieces), largest / len(pieces)))
        loudness = loudness * jnp.repeat(steps, extent[position] // shards_of).reshape([-1 if axis == position else 1 for axis in range(len(extent))])
    return loudness


def shared_out(stream_key, own, number, rows, amount, top, bound, lean):
    order = jax.random.permutation(stream_key, amount)
    heavy_load, ordinary = portions_of(amount, rows * top, bound, lean, True), portions_of(amount, rows * top, bound, lean, False)
    places = jnp.arange(amount)

    def named(sizes, offset_by):
        used = int((sizes > 0).sum())
        fixed = max(1, used // 4)
        shifted = fixed + (places - fixed + offset_by * (used - fixed)) % max(1, amount - fixed)
        return jnp.zeros((amount,), jnp.int32).at[order[jnp.where(places < fixed, places, shifted)]].set(jnp.asarray(sizes, jnp.int32))

    sizes = jnp.where(number % 4 == 0, named(heavy_load, number // 4), named(ordinary, number - number // 4 - 1))
    mixed = jax.random.permutation(jax.random.fold_in(own, 3), amount)
    donor, receiver = mixed[0:amount // 2 * 2:2], mixed[1:amount // 2 * 2:2]
    slack = jnp.minimum(sizes[donor] - 1, bound - sizes[receiver]) // 2
    slack = jnp.where((donor == order[0]) | (receiver == order[0]) | (sizes[receiver] == 0), 0, jnp.maximum(slack, 0))
    shifted = jax.random.randint(jax.random.fold_in(own, 4), (amount // 2,), 0, 1 << 20) % (slack + 1)
    sizes = sizes.at[donor].add(-shifted).at[receiver].add(shifted)
    labels = jnp.searchsorted(jnp.cumsum(sizes), jnp.arange(rows * top), side="right").astype(jnp.int32)
    grid = labels.reshape(top, rows).T
    grid = grid[jax.random.permutation(jax.random.fold_in(own, 1), rows)]
    offset_by = jax.random.randint(jax.random.fold_in(own, 2), (rows, 1), 0, top)
    return jnp.take_along_axis(grid, (jnp.arange(top)[None, :] + offset_by) % top, axis=1)


def portions_of(amount, total, bound, skew, full):
    portions = [(1 << 20) // math.isqrt(standing ** skew) + 1 for standing in range(1, amount + 1)]
    largest = bound if full else min(bound, max(-(-total // amount), total * portions[0] // sum(portions)))
    least = 1 if total - largest >= amount - 1 else 0
    counts, spare = [largest] + [least] * (amount - 1), total - largest - least * (amount - 1)
    while spare > 0:
        movable = [i for i in range(1, amount) if counts[i] < largest] or [i for i in range(1, amount) if counts[i] < bound]
        pool, remaining = sum([portions[i] for i in movable]), spare
        for i in movable:
            extra = min(bound - counts[i], max(1, remaining * portions[i] // pool), spare)
            counts[i] = counts[i] + extra
            spare = spare - extra
    return np.array(counts)


def centred(stream_key, shape, deviation, bound, cuts=(), kind=jnp.bfloat16):
    values = deviation * jax.random.normal(stream_key, shape, jnp.float32)
    if cuts:
        values = values * block_scale(stream_key, shape, cuts, -0.22, 0.18)
    return jnp.clip(values, -bound, bound).astype(kind)


def setup_inputs(seed: int = 0) -> dict:
    streams_of = jax.random.split(jax.random.key(seed), 14)
    q_nope = centred(streams_of[0], (SEQ, HEADS * NOPE), 1.0, 6.0, ((0, 32), (1, 4)))
    q_rope = draw_q_rope(jax.random.fold_in(streams_of[13], 71), 0)
    latent = centred(streams_of[2], (SEQ, LAT), 1.0, 6.0, ((0, 32),))
    k_rope = draw_k_rope(jax.random.fold_in(streams_of[13], 71), 0)
    w_uk = centred(streams_of[4], (LAT, HEADS * NOPE), LAT ** -0.5, 0.25, ((1, 4),))
    w_uv = centred(streams_of[5], (LAT, HEADS * VDIM), LAT ** -0.5, 0.25, ((1, 4),))
    positions = draw_positions(jax.random.fold_in(streams_of[13], 71), 0)
    moe_rows = centred(streams_of[7], (MOE_TOKENS, D), 1.0, 6.0, ((0, 32), (1, 4)))
    expert_ids_keys = jax.random.split(jax.random.fold_in(streams_of[8], 1), MOE_TOKENS // ROWS)
    expert_ids_turns = jax.random.permutation(jax.random.fold_in(streams_of[8], 3), MOE_TOKENS // ROWS)
    expert_ids = jax.vmap(lambda own, number: shared_out(jax.random.fold_in(streams_of[8], 2), own, number, ROWS, EXPERTS, TOP, CAP, 1))(expert_ids_keys, expert_ids_turns).reshape((MOE_TOKENS, TOP))
    expert_weights = jnp.clip(0.05 + 0.45 * jax.random.uniform(streams_of[9], (MOE_TOKENS, TOP), jnp.float32) ** block_scale(streams_of[9], (MOE_TOKENS, TOP), ((0, 32),), -0.2, 0.2), 0.05, 0.5)
    w_gate = centred(streams_of[10], (EXP_WIN, D, F), D ** -0.5, 0.0625, ((0, 32), (2, 4)))
    w_up = centred(streams_of[11], (EXP_WIN, D, F), D ** -0.5, 0.0625, ((0, 32), (2, 4)))
    w_down = centred(streams_of[12], (EXP_WIN, F, D), F ** -0.5, 0.1875, ((0, 32), (1, 4)))
    return dict(q_nope=q_nope, q_rope=q_rope, latent=latent, k_rope=k_rope, w_uk=w_uk, w_uv=w_uv, positions=positions, moe_rows=moe_rows, expert_ids=expert_ids, expert_weights=expert_weights, w_gate=w_gate, w_up=w_up, w_down=w_down)


def reference(q_nope, q_rope, latent, k_rope, w_uk, w_uv, positions, moe_rows, expert_ids, expert_weights, w_gate, w_up, w_down):
    seq_len = latent.shape[0]
    keys_nope = jnp.dot(latent, w_uk, preferred_element_type=jnp.float32).astype(jnp.bfloat16)
    values = jnp.dot(latent, w_uv, preferred_element_type=jnp.float32).astype(jnp.bfloat16)
    per_head = (q_nope.reshape(seq_len, HEADS, NOPE).transpose(1, 0, 2), q_rope.reshape(seq_len, HEADS, ROPE).transpose(1, 0, 2), keys_nope.reshape(seq_len, HEADS, NOPE).transpose(1, 0, 2), values.reshape(seq_len, HEADS, VDIM).transpose(1, 0, 2))
    visible = positions[None, :] <= positions[:, None]
    score_scale = 1.0 / math.sqrt(NOPE + ROPE)

    def one_head(operands):
        query_nope, query_rope, head_keys, head_values = operands
        scores = jnp.dot(query_nope, head_keys.T, preferred_element_type=jnp.float32)
        scores = (scores + jnp.dot(query_rope, k_rope.T, preferred_element_type=jnp.float32)) * score_scale
        scores = jnp.where(visible, scores, -jnp.inf)
        row_max = lax.optimization_barrier(jnp.max(scores, axis=1, keepdims=True))
        weights_exp = jnp.where(visible, jnp.exp(scores - row_max), 0.0)
        row_total = lax.optimization_barrier(jnp.sum(weights_exp, axis=1, keepdims=True))
        return jnp.dot(weights_exp.astype(jnp.bfloat16), head_values, preferred_element_type=jnp.float32) / row_total
    attended = lax.map(one_head, per_head)
    attention = attended.transpose(1, 0, 2).reshape(seq_len, HEADS * VDIM).astype(jnp.bfloat16)
    token_count = moe_rows.shape[0]
    flat_experts = expert_ids.reshape(N_CTX, ROWS * TOP)
    in_window = flat_experts < EXP_WIN
    one_hot = ((flat_experts[:, :, None] == jnp.arange(EXP_WIN, dtype=jnp.int32)[None, None, :]) & in_window[:, :, None]).astype(jnp.int32)
    earlier = jnp.cumsum(one_hot, axis=1) - one_hot
    rank_in_expert = lax.optimization_barrier(jnp.sum(earlier * one_hot, axis=2)).astype(jnp.int32)
    block_index = jnp.arange(N_CTX, dtype=jnp.int32)[:, None]
    capacity_rows = N_CTX * CAP
    slot_index = jnp.where(in_window, flat_experts * capacity_rows + block_index * CAP + rank_in_expert, EXP_WIN * capacity_rows).reshape(-1).astype(jnp.int32)
    token_index = jnp.repeat(jnp.arange(token_count, dtype=jnp.int32), TOP)
    source_rows = jnp.zeros((EXP_WIN * capacity_rows,), jnp.int32).at[slot_index].set(token_index, mode='drop')
    slot_weights = jnp.zeros((EXP_WIN * capacity_rows,), jnp.float32).at[slot_index].set(expert_weights.reshape(-1), mode='drop')

    def add_expert(total, operands):
        rows_of, weights_of, gate_mat, up_mat, down_mat = operands
        inputs = moe_rows[rows_of]
        gate = jnp.dot(inputs, gate_mat, preferred_element_type=jnp.float32)
        upper = jnp.dot(inputs, up_mat, preferred_element_type=jnp.float32)
        hidden = (jax.nn.silu(gate) * upper).astype(jnp.bfloat16)
        outputs = jnp.dot(hidden, down_mat, preferred_element_type=jnp.float32)
        return (total.at[rows_of].add(weights_of[:, None] * outputs), None)
    total, unused = lax.scan(add_expert, jnp.zeros((token_count, D), jnp.float32), (source_rows.reshape(EXP_WIN, capacity_rows), slot_weights.reshape(EXP_WIN, capacity_rows), w_gate, w_up, w_down))
    return (attention, total.astype(jnp.bfloat16))
```

```python
import math

import jax
import jax.numpy as jnp
from jax import lax
from jax.experimental import pallas as pl
from jax.experimental.pallas import tpu as pltpu
from jax.sharding import PartitionSpec as P

F32 = jnp.float32
BF16 = jnp.bfloat16
MESH = pl.DeviceIdType.MESH

NOPE = 128
ROPE = 64
LAT = 512
CAP = 8
N_CTX = 32
KW = LAT + 2 * ROPE
RUN = 64
GROUP = 256
SCALE = 1.0 / math.sqrt(NOPE + ROPE)
LOG2E = math.log2(math.e)
LOW = -1e30


def dot(a, b):
    return jnp.dot(a, b, preferred_element_type=F32)


def dot_t(a, b):
    return lax.dot_general(a, b, (((1,), (1,)), ((), ())), preferred_element_type=F32)


def iota(shape, dim):
    return lax.broadcasted_iota(jnp.int32, shape, dim)


def kernel(
    meta,
    latent,
    k_rope,
    rows,
    ids,
    weights,
    q_nope_h,
    q_rope_h,
    w_uk_h,
    w_uv_h,
    w_gate_h,
    w_up_h,
    w_down_h,
    attn_out,
    moe_out,
    q_nope,
    q_rope,
    w_uk,
    w_uv,
    w_gate,
    w_up,
    w_down,
    outgoing,
    slots,
    to_mate,
    from_mate,
    to_pair,
    kept,
    from_pair,
    going,
    returned,
    keys,
    key_group,
    queries,
    acc,
    row_max,
    row_sum,
    load_sem,
    disp_send,
    disp_recv,
    pair_send,
    pair_recv,
    core_send,
    core_recv,
    ag_send,
    ag_recv,
    back_core_send,
    back_core_recv,
    back_pair_send,
    back_pair_recv,
    back_send,
    back_recv,
):
    ctx = lax.axis_index("ctx")
    ep = lax.axis_index("ep")
    h = ctx // 16
    z = (ctx // 4) % 4
    y = ctx % 4
    lo = ep // 2
    core = ep % 2
    ep_pair = (1 - lo) * 2 + core
    ep_mate = lo * 2 + (1 - core)
    part = rows.shape[1]
    half = part // 2

    def context(step, dz, dy):
        other = h if step == 0 else 1 - h
        return other * 16 + ((z + dz) % 4) * 4 + (y + dy) % 4

    def partner_ep(step):
        return ep if step == 0 else ep_pair

    def window(step):
        return (h if step == 0 else 1 - h) * 16

    def kept_lo(step):
        return lo if step == 0 else 1 - lo

    order = [(s, dz, dy) for s in range(2) for dz in (0, 1, 3, 2) for dy in (0, 1, 3, 2)]

    loads = [
        pltpu.make_async_copy(src, dst, load_sem.at[i])
        for i, (src, dst) in enumerate(
            (
                (q_nope_h, q_nope),
                (q_rope_h, q_rope),
                (w_uk_h, w_uk),
                (w_gate_h.at[0], w_gate),
                (w_up_h.at[0], w_up),
                (w_down_h.at[0], w_down),
                (w_uv_h, w_uv),
            )
        )
    ]
    for load in loads:
        load.start()

    barrier = pltpu.get_barrier_semaphore()
    for s, dz, dy in order[1:]:
        pl.semaphore_signal(
            barrier, inc=1, device_id=(context(s, dz, dy), partner_ep(s)), device_id_type=MESH
        )
    pl.semaphore_signal(barrier, inc=1, device_id=(ctx, ep_pair), device_id_type=MESH)
    pl.semaphore_signal(barrier, inc=1, device_id=(ctx, ep_mate), device_id_type=MESH)

    lane = iota((128, 128), 1)
    named = jnp.zeros((128, 128), F32)
    slot_weight = jnp.zeros((128, 128), F32)
    for k in range(ids.shape[1]):
        hit = (ids[:, k : k + 1] == lane) & (lane < N_CTX)
        named = jnp.where(hit, 1.0, named)
        slot_weight = jnp.where(hit, weights[:, k : k + 1], slot_weight)
    earlier = jnp.where(lane < iota((128, 128), 0), 1.0, 0.0).astype(BF16)
    rank = dot(earlier, named.astype(BF16))
    named_b = named.astype(BF16)
    rank_b = rank.astype(BF16)
    spread = jnp.where(iota((256, 128), 0) // CAP == iota((256, 128), 1), 1.0, 0.0).astype(BF16)
    picked = (dot_t(spread, named_b) > 0.5) & (
        dot_t(spread, rank_b) == (iota((256, 128), 0) % CAP).astype(F32)
    )
    pick = jnp.where(picked, 1.0, 0.0).astype(BF16)
    for c in range(4):
        lhs = pick[64 * c : 64 * (c + 1)]
        first = dot(lhs, rows[:, :half]).reshape(8, CAP, half)
        second = dot(lhs, rows[:, half:]).reshape(8, CAP, half)
        outgoing[8 * c : 8 * (c + 1)] = jnp.concatenate([first, second], axis=1).astype(BF16)

    double = jnp.where(iota((64, 128), 1) % ROPE == iota((64, 128), 0), 1.0, 0.0).astype(BF16)
    own_rows = pl.ds(pl.multiple_of(core * RUN, RUN), RUN)
    major = jnp.where(core == 0, z, y)
    minor = jnp.where(core == 0, y, z)
    keys[core, h, major * 4 + minor, :, :LAT] = latent[own_rows, :]
    keys[core, h, major * 4 + minor, :, LAT:] = dot(k_rope[own_rows, :], double).astype(BF16)

    pl.semaphore_wait(barrier, 33)

    own = pltpu.make_async_copy(outgoing.at[ctx], slots.at[ep, ctx], disp_recv.at[0, 0])
    own.start()
    for s, dz, dy in order[1:]:
        to = context(s, dz, dy)
        pltpu.make_async_remote_copy(
            src_ref=outgoing.at[to],
            dst_ref=slots.at[ep, ctx],
            send_sem=disp_send.at[0],
            recv_sem=disp_recv.at[s, dz],
            device_id=(to, partner_ep(s)),
            device_id_type=MESH,
        ).start()

    def at_axis(major_to, minor_to):
        z_to = jnp.where(core == 0, major_to, minor_to)
        y_to = jnp.where(core == 0, minor_to, major_to)
        return h * 16 + z_to * 4 + y_to

    pltpu.make_async_remote_copy(
        src_ref=keys.at[core, h, major * 4 + minor],
        dst_ref=keys.at[core, h, major * 4 + minor],
        send_sem=ag_send.at[0],
        recv_sem=ag_recv.at[0],
        device_id=((1 - h) * 16 + z * 4 + y, ep_pair),
        device_id_type=MESH,
    ).start()

    def wait_for(ref, sem):
        pltpu.make_async_copy(ref, ref, sem).wait()

    for load in loads[:3]:
        load.wait()
    even = iota((1, 128), 1) < ROPE

    @pl.loop(0, 8)
    def _(pair):
        at = pl.ds(pl.multiple_of(pair * 128, 128), 128)
        rope = q_rope[:, at].astype(F32)
        for which in range(2):
            cols = pl.ds(pl.multiple_of(pair * 256 + which * 128, 128), 128)
            lat = dot_t(q_nope[:, cols], w_uk[:, cols]).astype(BF16)
            rot = jnp.where(even if which == 0 else ~even, rope, 0.0).astype(BF16)
            to = pl.ds(pl.multiple_of(pair * 128 + which * 64, 64), 64)
            for run in range(2):
                queries[run, to, :LAT] = lat[run * 64 : (run + 1) * 64]
                queries[run, to, LAT:] = rot[run * 64 : (run + 1) * 64]

    def chunk(step, dz, lo_part):
        return slots.at[lo_part * 2 + core, pl.ds(window(step) + ((z - dz + 4) % 4) * 4, 4)]

    def relay(step, dz):
        region = chunk(step, dz, kept_lo(step))
        wait_for(region, disp_recv.at[step, dz])
        pltpu.make_async_remote_copy(
            src_ref=region,
            dst_ref=region,
            send_sem=pair_send.at[0],
            recv_sem=pair_recv.at[step, dz],
            device_id=(ctx, ep_pair),
            device_id_type=MESH,
        ).start()
        pltpu.make_async_remote_copy(
            src_ref=region,
            dst_ref=region,
            send_sem=core_send.at[0],
            recv_sem=core_recv.at[0, step],
            device_id=(ctx, ep_mate),
            device_id_type=MESH,
        ).start()

    def relay_again(step, dz):
        region = chunk(step, dz, 1 - kept_lo(step))
        wait_for(region, pair_recv.at[step, dz])
        pltpu.make_async_remote_copy(
            src_ref=region,
            dst_ref=region,
            send_sem=core_send.at[0],
            recv_sem=core_recv.at[1, step],
            device_id=(ctx, ep_mate),
            device_id_type=MESH,
        ).start()

    def keys_second():
        wait_for(keys.at[core, 1 - h, major * 4 + minor], ag_recv.at[0])
        for t in (1, 3, 2):
            region = keys.at[core, :, major * 4 + minor]
            pltpu.make_async_remote_copy(
                src_ref=region,
                dst_ref=region,
                send_sem=ag_send.at[1],
                recv_sem=ag_recv.at[1],
                device_id=(at_axis(major, (minor + t) % 4), ep),
                device_id_type=MESH,
            ).start()

    def keys_to_mate(at):
        region = keys.at[core, :, pl.ds(at * 4, 4)]
        pltpu.make_async_remote_copy(
            src_ref=region,
            dst_ref=region,
            send_sem=ag_send.at[3],
            recv_sem=ag_recv.at[5],
            device_id=(ctx, ep_mate),
            device_id_type=MESH,
        ).start()

    def keys_third():
        wait_for(keys.at[core, :, pl.ds(0, 3)], ag_recv.at[1])
        region = keys.at[core, :, pl.ds(major * 4, 4)]
        for t in (1, 3, 2):
            pltpu.make_async_remote_copy(
                src_ref=region,
                dst_ref=region,
                send_sem=ag_send.at[2],
                recv_sem=ag_recv.at[1 + t],
                device_id=(at_axis((major + t) % 4, minor), ep),
                device_id_type=MESH,
            ).start()
        keys_to_mate(major)

    def keys_share(t):
        at = (major - t + 4) % 4
        wait_for(keys.at[core, :, pl.ds(at * 4, 4)], ag_recv.at[1 + t])
        keys_to_mate(at)

    relay(0, 0)
    keys_second()
    relay(0, 1)
    relay(0, 3)
    relay(0, 2)
    keys_third()
    for dz in (0, 1, 3, 2):
        relay(1, dz)
    for dz in (0, 1, 3, 2):
        relay_again(0, dz)
    for load in loads[3:]:
        load.wait()

    def from_experts(step):
        start = window(step)
        for j in range(2):
            lo_part = kept_lo(step) if j == 0 else 1 - kept_lo(step)
            wait_for(
                slots.at[lo_part * 2 + (1 - core), pl.ds(start, 16)], core_recv.at[j, step]
            )

        def some(p, carry):
            gate, up = carry
            taken = slots[p, pl.ds(start, 16)].astype(F32)
            for i in range(2):
                x = taken[:, CAP * i : CAP * (i + 1)].reshape(128, half).astype(BF16)
                at = pl.ds(pl.multiple_of(p * part + i * half, 128), half)
                gate = gate + dot(x, w_gate[at, :])
                up = up + dot(x, w_up[at, :])
            return gate, up

        width = w_gate.shape[1]
        gate, up = lax.fori_loop(
            0, 4, some, (jnp.zeros((128, width), F32), jnp.zeros((128, width), F32))
        )
        hidden = (gate / (1.0 + jnp.exp(-gate)) * up).astype(BF16)

        def through_down(p):
            both = []
            for i in range(2):
                at = pl.ds(pl.multiple_of(p * part + i * half, 128), half)
                both.append(dot(hidden, w_down[:, at]).reshape(16, CAP, half))
            return jnp.concatenate(both, axis=1)

        for j in range(2):
            lo_part = 1 - kept_lo(step) if j == 0 else kept_lo(step)
            to_mate[step, j] = through_down(lo_part * 2 + (1 - core)).astype(BF16)
            pltpu.make_async_remote_copy(
                src_ref=to_mate.at[step, j],
                dst_ref=from_mate.at[step, j],
                send_sem=back_core_send.at[step, j],
                recv_sem=back_core_recv.at[step, j],
                device_id=(ctx, ep_mate),
                device_id_type=MESH,
            ).start()
        mine = through_down((1 - kept_lo(step)) * 2 + core)
        wait_for(from_mate.at[step, 0], back_core_recv.at[step, 0])
        to_pair[step] = (mine + from_mate[step, 0].astype(F32)).astype(BF16)
        pltpu.make_async_remote_copy(
            src_ref=to_pair.at[step],
            dst_ref=from_pair.at[step],
            send_sem=back_pair_send.at[step],
            recv_sem=back_pair_recv.at[step],
            device_id=(ctx, ep_pair),
            device_id_type=MESH,
        ).start()
        mine = through_down(kept_lo(step) * 2 + core)
        wait_for(from_mate.at[step, 1], back_core_recv.at[step, 1])
        kept[step] = (mine + from_mate[step, 1].astype(F32)).astype(BF16)

    def send_back(step):
        wait_for(from_pair.at[step], back_pair_recv.at[step])
        going[step] = (kept[step].astype(F32) + from_pair[step].astype(F32)).astype(BF16)
        for s, dz, dy in order:
            if s != step:
                continue
            to = context(s, dz, dy)
            at = ((z + dz) % 4) * 4 + (y + dy) % 4
            if (s, dz, dy) == (0, 0, 0):
                pltpu.make_async_copy(going.at[0, at], returned.at[ctx], back_recv.at[0]).start()
                continue
            pltpu.make_async_remote_copy(
                src_ref=going.at[s, at],
                dst_ref=returned.at[ctx],
                send_sem=back_send.at[0],
                recv_sem=back_recv.at[s],
                device_id=(to, partner_ep(s)),
                device_id_type=MESH,
            ).start()

    run_0 = meta[64 + 2 * ctx]
    run_1 = meta[64 + 2 * ctx + 1]
    run_late = jnp.maximum(run_0, run_1)
    run_early = jnp.minimum(run_0, run_1)
    late_half = jnp.where(run_1 > run_0, 1, 0)
    late_steps = run_late // 4 + 1
    heads_rows = queries.shape[1]
    blocks = heads_rows // 256

    row_max[...] = jnp.full(row_max.shape, LOW, F32)
    row_sum[...] = jnp.zeros(row_sum.shape, F32)
    acc[...] = jnp.zeros(acc.shape, F32)

    def attend(i, kind):
        is_late = i < late_steps
        if kind == "late":
            side, group, q_half, q_run = 1, i, late_half, run_late
        elif kind == "early":
            side, group, q_half, q_run = 0, i - late_steps, 1 - late_half, run_early
        else:
            side = jnp.where(is_late, 1, 0)
            group = jnp.where(is_late, i, i - late_steps)
            q_half = jnp.where(is_late, late_half, 1 - late_half)
            q_run = jnp.where(is_late, run_late, run_early)
        for t in range(4):
            at = meta[group * 4 + t]
            key_group[t * RUN : (t + 1) * RUN, :] = keys[at // 32, (at // 16) % 2, at % 16]
        key_pos = group * GROUP + iota((256, 256), 1)
        query_pos = q_run * RUN + iota((256, 256), 0) % RUN
        for b in range(blocks):
            at = slice(b * 256, (b + 1) * 256)
            scores = dot_t(queries[q_half, at, :], key_group[...])
            if masked(kind):
                scores = jnp.where(key_pos <= query_pos, scores, LOW)
            old_max = row_max[side, at, :]
            new_max = jnp.maximum(old_max, jnp.max(scores, axis=1, keepdims=True))
            fade = jnp.exp2((old_max - new_max) * (SCALE * LOG2E))
            probs = jnp.exp2(
                (scores - jnp.concatenate([new_max, new_max], axis=1)) * (SCALE * LOG2E)
            )
            new_sum = row_sum[side, at, :] * fade + (probs[:, :128] + probs[:, 128:])
            new_acc = acc[side, at, :] * jnp.concatenate([fade] * 4, axis=1) + dot(
                probs.astype(BF16), key_group[:, :LAT]
            )
            if kind == "any":
                for to in range(2):
                    here = side == to
                    row_max[to, at, :] = jnp.where(here, new_max, row_max[to, at, :])
                    row_sum[to, at, :] = jnp.where(here, new_sum, row_sum[to, at, :])
                    acc[to, at, :] = jnp.where(here, new_acc, acc[to, at, :])
            else:
                row_max[side, at, :] = new_max
                row_sum[side, at, :] = new_sum
                acc[side, at, :] = new_acc

    def masked(kind):
        return kind != "late"

    from_experts(0)
    for dz in (0, 1, 3, 2):
        relay_again(1, dz)
    from_experts(1)
    keys_share(1)
    keys_share(3)
    keys_share(2)
    wait_for(keys.at[1 - core], ag_recv.at[5])

    @pl.loop(0, 4)
    def _(i):
        attend(i, "late")

    send_back(0)

    @pl.loop(4, 8)
    def _(i):
        attend(i, "late")

    @pl.loop(8, 12)
    def _(i):
        attend(i, "any")

    send_back(1)

    @pl.loop(12, 16)
    def _(i):
        attend(i, "any")

    attend(jnp.int32(16), "early")

    first_side = jnp.where(run_0 > run_1, 1, 0)

    @pl.loop(0, 16)
    def _(head):
        at = pl.ds(pl.multiple_of(head * 64, 64), 64)
        cols = pl.ds(pl.multiple_of(head * 128, 128), 128)
        both = []
        for side in (first_side, 1 - first_side):
            total = jnp.sum(row_sum[side, at, :], axis=1, keepdims=True)
            both.append(acc[side, at, :] / total)
        mixed = jnp.concatenate(both, axis=0).astype(BF16)
        attn_out[:, cols] = dot(mixed, w_uv[:, cols]).astype(BF16)

    wide = (128, N_CTX * 2 * CAP)
    column = iota(wide, 1)
    spread_2 = jnp.where(column // (2 * CAP) == iota(wide, 0), 1.0, 0.0).astype(BF16)
    weight_hi = slot_weight.astype(BF16)
    weight_lo = (slot_weight - weight_hi.astype(F32)).astype(BF16)
    here = (dot(named_b, spread_2) > 0.5) & (
        dot(rank_b, spread_2) == (column % CAP).astype(F32)
    )
    parts = [dot(w, spread_2) for w in (weight_hi, weight_lo)]
    wait_for(returned.at[pl.ds(0, 16)], back_recv.at[0])
    wait_for(returned.at[pl.ds(0, 16)], back_recv.at[1])
    for i in range(2):
        mine = here & ((column // CAP) % 2 == i)
        total = jnp.zeros((128, half), F32)
        for w in parts:
            factor = jnp.where(mine, w, 0.0).astype(BF16)
            total = total + dot(factor, returned[...].reshape(N_CTX * 2 * CAP, half))
        moe_out[:, i * half : (i + 1) * half] = total.astype(BF16)

    wait_for(outgoing.at[pl.ds(0, 31)], disp_send.at[0])
    wait_for(slots.at[0], pair_send.at[0])
    wait_for(slots.at[pl.ds(0, 2)], core_send.at[0])
    wait_for(keys.at[0, 0, 0], ag_send.at[0])
    wait_for(keys.at[0, :, pl.ds(0, 3)], ag_send.at[1])
    wait_for(keys.at[0, :, pl.ds(0, 12)], ag_send.at[2])
    wait_for(keys.at[0], ag_send.at[3])
    for step in range(2):
        for j in range(2):
            wait_for(to_mate.at[step, j], back_core_send.at[step, j])
        wait_for(to_pair.at[step], back_pair_send.at[step])
    wait_for(outgoing.at[pl.ds(0, 31)], back_send.at[0])


def shards(
    q_nope,
    q_rope,
    latent,
    k_rope,
    w_uk,
    w_uv,
    positions,
    moe_rows,
    expert_ids,
    expert_weights,
    w_gate,
    w_up,
    w_down,
):
    runs = positions[::RUN] // RUN
    pairs = runs.reshape(N_CTX, 2)
    placed = jnp.concatenate(
        [pairs[:, 0], pairs[:, 1].reshape(2, 4, 4).transpose(0, 2, 1).reshape(N_CTX)]
    )
    spots = jnp.arange(2 * N_CTX, dtype=jnp.int32)
    where = jnp.sum(jnp.where(placed[None, :] == spots[:, None], spots[None, :], 0), axis=1)
    meta = jnp.concatenate([where, runs]).astype(jnp.int32)

    count, part = moe_rows.shape
    half = part // 2
    vmem = pl.BlockSpec(memory_space=pltpu.VMEM)
    anywhere = pl.BlockSpec(memory_space=pl.ANY)
    dma = pltpu.SemaphoreType.DMA
    heads_rows = q_nope.shape[1] // NOPE * RUN
    slot = (2 * CAP, half)
    return pl.pallas_call(
        kernel,
        out_shape=(
            jax.ShapeDtypeStruct(q_nope.shape, BF16),
            jax.ShapeDtypeStruct(moe_rows.shape, BF16),
        ),
        in_specs=[pl.BlockSpec(memory_space=pltpu.SMEM)] + [vmem] * 5 + [anywhere] * 7,
        out_specs=(vmem, vmem),
        scratch_shapes=[
            pltpu.VMEM(q_nope.shape, BF16),
            pltpu.VMEM(q_rope.shape, BF16),
            pltpu.VMEM(w_uk.shape, BF16),
            pltpu.VMEM(w_uv.shape, BF16),
            pltpu.VMEM(w_gate.shape[1:], BF16),
            pltpu.VMEM(w_up.shape[1:], BF16),
            pltpu.VMEM(w_down.shape[1:], BF16),
            pltpu.VMEM((N_CTX,) + slot, BF16),
            pltpu.VMEM((4, N_CTX) + slot, BF16),
            pltpu.VMEM((2, 2, 16) + slot, BF16),
            pltpu.VMEM((2, 2, 16) + slot, BF16),
            pltpu.VMEM((2, 16) + slot, BF16),
            pltpu.VMEM((2, 16) + slot, BF16),
            pltpu.VMEM((2, 16) + slot, BF16),
            pltpu.VMEM((2, 16) + slot, BF16),
            pltpu.VMEM((N_CTX,) + slot, BF16),
            pltpu.VMEM((2, 2, 16, RUN, KW), BF16),
            pltpu.VMEM((GROUP, KW), BF16),
            pltpu.VMEM((2, heads_rows, KW), BF16),
            pltpu.VMEM((2, heads_rows, LAT), F32),
            pltpu.VMEM((2, heads_rows, 128), F32),
            pltpu.VMEM((2, heads_rows, 128), F32),
            dma((7,)),
            dma((1,)),
            dma((2, 4)),
            dma((1,)),
            dma((2, 4)),
            dma((1,)),
            dma((2, 2)),
            dma((4,)),
            dma((6,)),
            dma((2, 2)),
            dma((2, 2)),
            dma((2,)),
            dma((2,)),
            dma((1,)),
            dma((2,)),
        ],
        compiler_params=pltpu.CompilerParams(
            collective_id=0, has_side_effects=True, vmem_limit_bytes=56 * 1024 * 1024
        ),
        name="attend_and_dispatch",
    )(
        meta,
        latent,
        k_rope,
        moe_rows,
        expert_ids,
        expert_weights,
        q_nope,
        q_rope,
        w_uk,
        w_uv,
        w_gate,
        w_up,
        w_down,
    )


def solution(mesh):
    return jax.shard_map(
        shards,
        mesh=mesh,
        in_specs=(
            P("ctx", "ep"),
            P("ctx", "ep"),
            P("ctx", None),
            P("ctx", None),
            P(None, "ep"),
            P(None, "ep"),
            P(),
            P("ctx", "ep"),
            P("ctx", None),
            P("ctx", None),
            P("ctx", None, "ep"),
            P("ctx", None, "ep"),
            P("ctx", "ep", None),
        ),
        out_specs=(P("ctx", "ep"), P("ctx", "ep")),
        check_vma=False,
    )
```

```python
import math

import jax
import jax.numpy as jnp
from jax import lax
from jax.experimental import pallas as pl
from jax.experimental.pallas import tpu as pltpu
from jax.sharding import PartitionSpec as P

F32 = jnp.float32
BF16 = jnp.bfloat16
MESH = pl.DeviceIdType.MESH

NOPE = 128
ROPE = 64
LAT = 512
CAP = 8
N_CTX = 32
KW = LAT + 2 * ROPE
RUN = 64
GROUP = 256
BLOCK = 512
SCALE = 1.0 / math.sqrt(NOPE + ROPE)
LOG2E = math.log2(math.e)
LOW = -1e30


def dot(a, b):
    return jnp.dot(a, b, preferred_element_type=F32)


def dot_t(a, b):
    return lax.dot_general(a, b, (((1,), (1,)), ((), ())), preferred_element_type=F32)


def dot_0(a, b):
    return lax.dot_general(a, b, (((0,), (0,)), ((), ())), preferred_element_type=F32)


def iota(shape, dim):
    return lax.broadcasted_iota(jnp.int32, shape, dim)


def kernel(
    positions_h,
    latent_h,
    k_rope_h,
    rows_h,
    ids_h,
    weights_h,
    q_nope_h,
    q_rope_h,
    w_uk_h,
    w_uv_h,
    w_gate_h,
    w_up_h,
    w_down_h,
    attn_out,
    moe_out,
    positions,
    latent,
    k_rope,
    rows,
    ids,
    weights,
    q_nope,
    q_rope,
    w_uk,
    w_gate,
    w_up,
    w_down,
    index_row,
    meta,
    outgoing,
    slots,
    to_mate,
    from_mate,
    to_pair,
    kept,
    from_pair,
    returned,
    keys,
    key_group,
    value_group,
    queries,
    acc,
    row_max,
    row_sum,
    mixed,
    load_sem,
    disp_send,
    disp_recv,
    pair_send,
    pair_recv,
    core_send,
    core_recv,
    ag_send,
    ag_recv,
    back_core_send,
    back_core_recv,
    back_pair_send,
    back_pair_recv,
    back_send,
    back_recv,
):
    ctx = lax.axis_index("ctx")
    ep = lax.axis_index("ep")
    h = ctx // 16
    z = (ctx // 4) % 4
    y = ctx % 4
    lo = ep // 2
    core = ep % 2
    ep_pair = (1 - lo) * 2 + core
    ep_mate = lo * 2 + (1 - core)
    part = rows.shape[1]
    half = part // 2

    def context(step, dz, dy):
        other = h if step == 0 else 1 - h
        return other * 16 + ((z + dz) % 4) * 4 + (y + dy) % 4

    def partner_ep(step):
        return ep if step == 0 else ep_pair

    def window(step):
        return (h if step == 0 else 1 - h) * 16

    def kept_lo(step):
        return lo if step == 0 else 1 - lo

    order = [(s, dz, dy) for s in range(2) for dz in (0, 1, 3, 2) for dy in (0, 1, 3, 2)]

    loads = [
        pltpu.make_async_copy(src, dst, load_sem.at[i])
        for i, (src, dst) in enumerate(
            (
                (ids_h, ids),
                (weights_h, weights),
                (rows_h, rows),
                (k_rope_h, k_rope),
                (latent_h, latent),
                (positions_h, positions),
                (q_nope_h, q_nope),
                (q_rope_h, q_rope),
                (w_uk_h, w_uk),
                (w_gate_h.at[0], w_gate),
                (w_up_h.at[0], w_up),
                (w_down_h.at[0], w_down),
            )
        )
    ]
    for load in loads[:9]:
        load.start()

    barrier = pltpu.get_barrier_semaphore()
    for s, dz, dy in order[1:]:
        pl.semaphore_signal(
            barrier, inc=1, device_id=(context(s, dz, dy), partner_ep(s)), device_id_type=MESH
        )
    pl.semaphore_signal(barrier, inc=1, device_id=(ctx, ep_pair), device_id_type=MESH)
    pl.semaphore_signal(barrier, inc=1, device_id=(ctx, ep_mate), device_id_type=MESH)

    for load in loads[:3]:
        load.wait()
    expert = iota((128, 128), 0)
    named = jnp.zeros((128, 128), F32)
    slot_weight = jnp.zeros((128, 128), F32)
    for k in range(ids.shape[0]):
        hit = (ids[k : k + 1, :] == expert) & (expert < N_CTX)
        named = jnp.where(hit, 1.0, named)
        slot_weight = jnp.where(hit, weights[k : k + 1, :], slot_weight)
    earlier = jnp.where(expert < iota((128, 128), 1), 1.0, 0.0).astype(BF16)
    named_b = named.astype(BF16)
    rank_b = dot(named_b, earlier).astype(BF16)
    spread = jnp.where(iota((256, 128), 0) // CAP == iota((256, 128), 1), 1.0, 0.0).astype(BF16)
    picked = (dot(spread, named_b) > 0.5) & (
        dot(spread, rank_b) == (iota((256, 128), 0) % CAP).astype(F32)
    )
    pick = jnp.where(picked, 1.0, 0.0).astype(BF16)
    for c in range(4):
        lhs = pick[64 * c : 64 * (c + 1)]
        first = dot(lhs, rows[:, :half]).reshape(8, CAP, half)
        second = dot(lhs, rows[:, half:]).reshape(8, CAP, half)
        outgoing[8 * c : 8 * (c + 1)] = jnp.concatenate([first, second], axis=1).astype(BF16)

    for load in loads[3:6]:
        load.wait()
    double = jnp.where(iota((ROPE, 128), 1) % ROPE == iota((ROPE, 128), 0), 1.0, 0.0).astype(BF16)
    own_rows = pl.ds(pl.multiple_of(core * RUN, RUN), RUN)
    major = jnp.where(core == 0, z, y)
    minor = jnp.where(core == 0, y, z)
    rotated = dot_0(k_rope[...], double)
    keys[core, h, major * 4 + minor, :, :LAT] = latent[own_rows, :]
    keys[core, h, major * 4 + minor, :, LAT:] = jnp.where(
        core == 0, rotated[:RUN], rotated[RUN:]
    ).astype(BF16)

    pl.semaphore_wait(barrier, 33)

    own = pltpu.make_async_copy(outgoing.at[ctx], slots.at[ep, ctx], disp_recv.at[0, 0])
    own.start()
    for s, dz, dy in order[1:]:
        to = context(s, dz, dy)
        pltpu.make_async_remote_copy(
            src_ref=outgoing.at[to],
            dst_ref=slots.at[ep, ctx],
            send_sem=disp_send.at[0],
            recv_sem=disp_recv.at[s, dz],
            device_id=(to, partner_ep(s)),
            device_id_type=MESH,
        ).start()

    def at_axis(major_to, minor_to):
        z_to = jnp.where(core == 0, major_to, minor_to)
        y_to = jnp.where(core == 0, minor_to, major_to)
        return h * 16 + z_to * 4 + y_to

    pltpu.make_async_remote_copy(
        src_ref=keys.at[core, h, major * 4 + minor],
        dst_ref=keys.at[core, h, major * 4 + minor],
        send_sem=ag_send.at[0],
        recv_sem=ag_recv.at[0],
        device_id=((1 - h) * 16 + z * 4 + y, ep_pair),
        device_id_type=MESH,
    ).start()

    def wait_for(ref, sem):
        pltpu.make_async_copy(ref, ref, sem).wait()

    block = iota((N_CTX, 128), 0)
    place_1 = N_CTX + (block // 16) * 16 + (block % 4) * 4 + (block // 4) % 4
    held_0 = positions[:, 0:1] // RUN == iota((N_CTX, 128), 1)
    held_1 = positions[:, RUN : RUN + 1] // RUN == iota((N_CTX, 128), 1)
    where = jnp.sum(jnp.where(held_0, block, 0) + jnp.where(held_1, place_1, 0), axis=0)
    index_row[...] = jnp.zeros(index_row.shape, jnp.int32)
    index_row[0:1, :] = where.reshape(1, 128)
    index_row[1:2, :] = positions[pl.ds(ctx, 1), :]
    index_copy = pltpu.make_async_copy(index_row, meta, load_sem.at[0])
    index_copy.start()

    for load in loads[6:9]:
        load.wait()
    for load in loads[9:]:
        load.start()
    unit = jnp.where(iota((128, 128), 0) == iota((128, 128), 1), 1.0, 0.0).astype(BF16)

    @pl.loop(0, 8)
    def _(pair):
        at = pl.ds(pl.multiple_of(pair * 128, 128), 128)
        cols = pl.ds(pl.multiple_of(pair * 256, 256), 256)
        for run in range(2):
            of_run = slice(run * RUN, (run + 1) * RUN)
            both = q_nope[of_run, cols].astype(F32)
            first = iota(both.shape, 1) < NOPE
            apart = jnp.concatenate(
                [jnp.where(first, both, 0.0), jnp.where(first, 0.0, both)], axis=0
            ).astype(BF16)
            queries[run, :LAT, at] = dot_t(w_uk[:, cols], apart).astype(BF16)
            both = q_rope[of_run, at].astype(F32)
            first = iota(both.shape, 1) < ROPE
            apart = jnp.concatenate(
                [jnp.where(first, both, 0.0), jnp.where(first, 0.0, both)], axis=0
            ).astype(BF16)
            queries[run, LAT:, at] = dot_t(unit, apart).astype(BF16)

    index_copy.wait()
    out_weights = pltpu.make_async_copy(w_uv_h, w_uk, load_sem.at[1])
    out_weights.start()

    def chunk(step, dz, lo_part):
        return slots.at[lo_part * 2 + core, pl.ds(window(step) + ((z - dz + 4) % 4) * 4, 4)]

    def relay(step, dz):
        region = chunk(step, dz, kept_lo(step))
        wait_for(region, disp_recv.at[step, dz])
        pltpu.make_async_remote_copy(
            src_ref=region,
            dst_ref=region,
            send_sem=pair_send.at[0],
            recv_sem=pair_recv.at[step, dz],
            device_id=(ctx, ep_pair),
            device_id_type=MESH,
        ).start()
        pltpu.make_async_remote_copy(
            src_ref=region,
            dst_ref=region,
            send_sem=core_send.at[0],
            recv_sem=core_recv.at[0, step],
            device_id=(ctx, ep_mate),
            device_id_type=MESH,
        ).start()

    def relay_again(step, dz):
        region = chunk(step, dz, 1 - kept_lo(step))
        wait_for(region, pair_recv.at[step, dz])
        pltpu.make_async_remote_copy(
            src_ref=region,
            dst_ref=region,
            send_sem=core_send.at[0],
            recv_sem=core_recv.at[1, step],
            device_id=(ctx, ep_mate),
            device_id_type=MESH,
        ).start()

    def keys_second():
        wait_for(keys.at[core, 1 - h, major * 4 + minor], ag_recv.at[0])
        for t in (1, 3, 2):
            region = keys.at[core, :, major * 4 + minor]
            pltpu.make_async_remote_copy(
                src_ref=region,
                dst_ref=region,
                send_sem=ag_send.at[1],
                recv_sem=ag_recv.at[1],
                device_id=(at_axis(major, (minor + t) % 4), ep),
                device_id_type=MESH,
            ).start()

    def keys_to_mate(at):
        region = keys.at[core, :, pl.ds(at * 4, 4)]
        pltpu.make_async_remote_copy(
            src_ref=region,
            dst_ref=region,
            send_sem=ag_send.at[3],
            recv_sem=ag_recv.at[5],
            device_id=(ctx, ep_mate),
            device_id_type=MESH,
        ).start()

    def keys_third():
        wait_for(keys.at[core, :, pl.ds(0, 3)], ag_recv.at[1])
        region = keys.at[core, :, pl.ds(major * 4, 4)]
        for t in (1, 3, 2):
            pltpu.make_async_remote_copy(
                src_ref=region,
                dst_ref=region,
                send_sem=ag_send.at[2],
                recv_sem=ag_recv.at[1 + t],
                device_id=(at_axis((major + t) % 4, minor), ep),
                device_id_type=MESH,
            ).start()
        keys_to_mate(major)

    def keys_share(t):
        at = (major - t + 4) % 4
        wait_for(keys.at[core, :, pl.ds(at * 4, 4)], ag_recv.at[1 + t])
        keys_to_mate(at)

    relay(0, 0)
    keys_second()
    relay(0, 1)
    relay(0, 3)
    relay(0, 2)
    keys_third()
    for dz in (0, 1, 3, 2):
        relay(1, dz)
    for dz in (0, 1, 3, 2):
        relay_again(0, dz)
    for load in loads[9:]:
        load.wait()
    wait_for(outgoing.at[pl.ds(0, 31)], disp_send.at[0])

    def from_experts(step):
        start = window(step)
        for j in range(2):
            lo_part = kept_lo(step) if j == 0 else 1 - kept_lo(step)
            wait_for(
                slots.at[lo_part * 2 + (1 - core), pl.ds(start, 16)], core_recv.at[j, step]
            )

        def some(p, carry):
            gate, up = carry
            taken = slots[p, pl.ds(start, 16)].astype(F32)
            for i in range(2):
                x = taken[:, CAP * i : CAP * (i + 1)].reshape(128, half).astype(BF16)
                at = pl.ds(pl.multiple_of(p * part + i * half, 128), half)
                gate = gate + dot(x, w_gate[at, :])
                up = up + dot(x, w_up[at, :])
            return gate, up

        width = w_gate.shape[1]
        gate, up = lax.fori_loop(
            0, 4, some, (jnp.zeros((128, width), F32), jnp.zeros((128, width), F32))
        )
        hidden = (gate / (1.0 + jnp.exp(-gate)) * up).astype(BF16)

        def through_down(p):
            both = []
            for i in range(2):
                at = pl.ds(pl.multiple_of(p * part + i * half, 128), half)
                both.append(dot(hidden, w_down[:, at]).reshape(16, CAP, half))
            return jnp.concatenate(both, axis=1)

        for j in range(2):
            lo_part = 1 - kept_lo(step) if j == 0 else kept_lo(step)
            to_mate[step, j] = through_down(lo_part * 2 + (1 - core)).astype(BF16)
            pltpu.make_async_remote_copy(
                src_ref=to_mate.at[step, j],
                dst_ref=from_mate.at[step, j],
                send_sem=back_core_send.at[step, j],
                recv_sem=back_core_recv.at[step, j],
                device_id=(ctx, ep_mate),
                device_id_type=MESH,
            ).start()
        mine = through_down((1 - kept_lo(step)) * 2 + core)
        wait_for(from_mate.at[step, 0], back_core_recv.at[step, 0])
        to_pair[step] = (mine + from_mate[step, 0].astype(F32)).astype(BF16)
        for dz in (0, 1, 3, 2):
            some_of = pl.ds(((z + dz) % 4) * 4, 4)
            pltpu.make_async_remote_copy(
                src_ref=to_pair.at[step, some_of],
                dst_ref=from_pair.at[step, some_of],
                send_sem=back_pair_send.at[step],
                recv_sem=back_pair_recv.at[step, dz],
                device_id=(ctx, ep_pair),
                device_id_type=MESH,
            ).start()
        mine = through_down(kept_lo(step) * 2 + core)
        wait_for(from_mate.at[step, 1], back_core_recv.at[step, 1])
        kept[step] = (mine + from_mate[step, 1].astype(F32)).astype(BF16)

    def send_back(step, dz):
        start = ((z + dz) % 4) * 4
        some_of = pl.ds(start, 4)
        wait_for(from_pair.at[step, some_of], back_pair_recv.at[step, dz])
        base = window(step) + start
        outgoing[pl.ds(base, 4)] = (
            kept[step, some_of].astype(F32) + from_pair[step, some_of].astype(F32)
        ).astype(BF16)
        for dy in (0, 1, 3, 2):
            to = base + (y + dy) % 4

            def send(to=to):
                pltpu.make_async_remote_copy(
                    src_ref=outgoing.at[to],
                    dst_ref=returned.at[ctx],
                    send_sem=back_send.at[0],
                    recv_sem=back_recv.at[step],
                    device_id=(to, partner_ep(step)),
                    device_id_type=MESH,
                ).start()

            if step == 0 and dy == 0:
                pl.when(dz != 0)(send)

                @pl.when(dz == 0)
                def _():
                    pltpu.make_async_copy(
                        outgoing.at[ctx], returned.at[ctx], back_recv.at[0]
                    ).start()

            else:
                send()

    run_0 = meta[1, 0] // RUN
    run_1 = meta[1, RUN] // RUN
    run_late = jnp.maximum(run_0, run_1)
    run_early = jnp.minimum(run_0, run_1)
    late_half = jnp.where(run_1 > run_0, 1, 0)
    late_steps = run_late // 4 + 1
    columns = queries.shape[2]

    def take_keys(group, count):
        for t in range(count // RUN):
            at = jnp.clip(meta[0, group * 4 + t], 0, 2 * N_CTX - 1)
            key_group[t * RUN : (t + 1) * RUN, :] = keys[at // 32, (at // 16) % 2, at % 16]
        for t in range(count // 128):
            at = slice(t * 128, (t + 1) * 128)
            value_group[:, at] = key_group[at, :LAT].T

    def attend(i, wide):
        if wide:
            count, group, q_half = 2 * GROUP, 2 * i, late_half
        else:
            is_late = i < late_steps
            count = GROUP
            group = jnp.where(is_late, i, i - late_steps)
            q_half = jnp.where(is_late, late_half, 1 - late_half)
            q_run = jnp.where(is_late, run_late, run_early)
            turn = i == late_steps
        take_keys(group, count)

        def scores_of(b):
            scores = dot(
                key_group[:count, :], queries[q_half, :, b * BLOCK : (b + 1) * BLOCK]
            )
            if not wide:
                key_pos = group * GROUP + iota(scores.shape, 0)
                query_pos = q_run * RUN + iota(scores.shape, 1) % RUN
                scores = jnp.where(key_pos <= query_pos, scores, LOW)
            return scores

        following = scores_of(0)
        for b in range(columns // BLOCK):
            at = slice(b * BLOCK, (b + 1) * BLOCK)
            scores = following
            if (b + 1) * BLOCK < columns:
                following = scores_of(b + 1)
            old_max = row_max[:, at]
            if not wide:
                old_max = jnp.where(turn, LOW, old_max)
            new_max = jnp.maximum(old_max, jnp.max(scores, axis=0, keepdims=True))
            fade = jnp.exp2((old_max - new_max) * (SCALE * LOG2E))
            probs = jnp.exp2((scores - new_max[:1]) * (SCALE * LOG2E))
            new_sum = row_sum[:, at] * fade + jnp.sum(
                probs.reshape(count // 8, 8, BLOCK), axis=0
            )
            new_acc = acc[:, at] * fade[:1] + dot(value_group[:, :count], probs.astype(BF16))
            row_max[:, at] = new_max
            row_sum[:, at] = new_sum
            acc[:, at] = new_acc
            if not wide:
                whole = jnp.sum(new_sum, axis=0, keepdims=True)
                mixed[i - 8, :, at] = (new_acc * (1.0 / whole)).astype(BF16)

    row_max[...] = jnp.full(row_max.shape, LOW, F32)
    row_sum[...] = jnp.zeros(row_sum.shape, F32)
    acc[...] = jnp.zeros(acc.shape, F32)

    from_experts(0)
    for dz in (0, 1, 3, 2):
        relay_again(1, dz)
    from_experts(1)
    keys_share(1)
    keys_share(3)
    keys_share(2)
    wait_for(keys.at[1 - core], ag_recv.at[5])

    def gray(i):
        return jnp.where(i < 2, i, 5 - i)

    @pl.loop(0, 4)
    def _(i):
        attend(i, True)
        send_back(0, gray(i))

    @pl.loop(0, 4)
    def _(i):
        attend(8 + 2 * i, False)
        attend(9 + 2 * i, False)
        send_back(1, gray(i))

    attend(jnp.int32(16), False)

    out_weights.wait()
    late_at = jnp.clip(late_steps - 9, 0, 7)

    @pl.loop(0, 8)
    def _(pair):
        at = pl.ds(pl.multiple_of(pair * 128, 128), 128)
        for run in range(2):
            place = jnp.where(late_half == run, late_at, 8)
            cols = pl.ds(pl.multiple_of(pair * 256, 256), 256)
            both = dot_0(mixed[place, :, at], w_uk[:, cols])
            for i in range(2):
                to = pl.ds(pl.multiple_of(pair * 256 + i * 128, 128), 128)
                attn_out[run * RUN : (run + 1) * RUN, to] = both[
                    i * RUN : (i + 1) * RUN, i * 128 : (i + 1) * 128
                ].astype(BF16)

    wide = (128, N_CTX * 2 * CAP)
    column = iota(wide, 1)
    spread_2 = jnp.where(column // (2 * CAP) == iota(wide, 0), 1.0, 0.0).astype(BF16)
    weight_hi = slot_weight.astype(BF16)
    weight_lo = (slot_weight - weight_hi.astype(F32)).astype(BF16)
    here = (dot_0(named_b, spread_2) > 0.5) & (
        dot_0(rank_b, spread_2) == (column % CAP).astype(F32)
    )
    parts = [dot_0(w, spread_2) for w in (weight_hi, weight_lo)]
    wait_for(returned.at[pl.ds(0, 16)], back_recv.at[0])
    wait_for(returned.at[pl.ds(0, 16)], back_recv.at[1])
    for i in range(2):
        mine = here & ((column // CAP) % 2 == i)
        total = jnp.zeros((128, half), F32)
        for w in parts:
            factor = jnp.where(mine, w, 0.0).astype(BF16)
            total = total + dot(factor, returned[...].reshape(N_CTX * 2 * CAP, half))
        moe_out[:, i * half : (i + 1) * half] = total.astype(BF16)

    wait_for(slots.at[0], pair_send.at[0])
    wait_for(slots.at[pl.ds(0, 2)], core_send.at[0])
    wait_for(keys.at[0, 0, 0], ag_send.at[0])
    wait_for(keys.at[0, :, pl.ds(0, 3)], ag_send.at[1])
    wait_for(keys.at[0, :, pl.ds(0, 12)], ag_send.at[2])
    wait_for(keys.at[0], ag_send.at[3])
    for step in range(2):
        for j in range(2):
            wait_for(to_mate.at[step, j], back_core_send.at[step, j])
        wait_for(to_pair.at[step], back_pair_send.at[step])
    wait_for(outgoing.at[pl.ds(0, 31)], back_send.at[0])


def shards(
    q_nope,
    q_rope,
    latent,
    k_rope,
    w_uk,
    w_uv,
    positions,
    moe_rows,
    expert_ids,
    expert_weights,
    w_gate,
    w_up,
    w_down,
):
    count, part = moe_rows.shape
    half = part // 2
    vmem = pl.BlockSpec(memory_space=pltpu.VMEM)
    anywhere = pl.BlockSpec(memory_space=pl.ANY)
    dma = pltpu.SemaphoreType.DMA
    columns = q_nope.shape[1] // NOPE * RUN
    slot = (2 * CAP, half)
    return pl.pallas_call(
        kernel,
        out_shape=(
            jax.ShapeDtypeStruct(q_nope.shape, BF16),
            jax.ShapeDtypeStruct(moe_rows.shape, BF16),
        ),
        in_specs=[anywhere] * 13,
        out_specs=(vmem, vmem),
        scratch_shapes=[
            pltpu.VMEM((N_CTX, count), jnp.int32),
            pltpu.VMEM(latent.shape, BF16),
            pltpu.VMEM(k_rope.shape[::-1], BF16),
            pltpu.VMEM(moe_rows.shape, BF16),
            pltpu.VMEM(expert_ids.shape[::-1], jnp.int32),
            pltpu.VMEM(expert_weights.shape[::-1], F32),
            pltpu.VMEM(q_nope.shape, BF16),
            pltpu.VMEM(q_rope.shape, BF16),
            pltpu.VMEM(w_uk.shape, BF16),
            pltpu.VMEM(w_gate.shape[1:], BF16),
            pltpu.VMEM(w_up.shape[1:], BF16),
            pltpu.VMEM(w_down.shape[1:], BF16),
            pltpu.VMEM((8, 128), jnp.int32),
            pltpu.SMEM((8, 128), jnp.int32),
            pltpu.VMEM((N_CTX,) + slot, BF16),
            pltpu.VMEM((4, N_CTX) + slot, BF16),
            pltpu.VMEM((2, 2, 16) + slot, BF16),
            pltpu.VMEM((2, 2, 16) + slot, BF16),
            pltpu.VMEM((2, 16) + slot, BF16),
            pltpu.VMEM((2, 16) + slot, BF16),
            pltpu.VMEM((2, 16) + slot, BF16),
            pltpu.VMEM((N_CTX,) + slot, BF16),
            pltpu.VMEM((2, 2, 16, RUN, KW), BF16),
            pltpu.VMEM((2 * GROUP, KW), BF16),
            pltpu.VMEM((LAT, 2 * GROUP), BF16),
            pltpu.VMEM((2, KW, columns), BF16),
            pltpu.VMEM((LAT, columns), F32),
            pltpu.VMEM((8, columns), F32),
            pltpu.VMEM((8, columns), F32),
            pltpu.VMEM((9, LAT, columns), BF16),
            dma((12,)),
            dma((1,)),
            dma((2, 4)),
            dma((1,)),
            dma((2, 4)),
            dma((1,)),
            dma((2, 2)),
            dma((4,)),
            dma((6,)),
            dma((2, 2)),
            dma((2, 2)),
            dma((2,)),
            dma((2, 4)),
            dma((1,)),
            dma((2,)),
        ],
        compiler_params=pltpu.CompilerParams(
            collective_id=0, has_side_effects=True, vmem_limit_bytes=56 * 1024 * 1024
        ),
        name="attend_and_dispatch",
    )(
        positions.reshape(N_CTX, count),
        latent,
        k_rope.T,
        moe_rows,
        expert_ids.T,
        expert_weights.T,
        q_nope,
        q_rope,
        w_uk,
        w_uv,
        w_gate,
        w_up,
        w_down,
    )


def solution(mesh):
    return jax.shard_map(
        shards,
        mesh=mesh,
        in_specs=(
            P("ctx", "ep"),
            P("ctx", "ep"),
            P("ctx", None),
            P("ctx", None),
            P(None, "ep"),
            P(None, "ep"),
            P(),
            P("ctx", "ep"),
            P("ctx", None),
            P("ctx", None),
            P("ctx", None, "ep"),
            P("ctx", None, "ep"),
            P("ctx", "ep", None),
        ),
        out_specs=(P("ctx", "ep"), P("ctx", "ep")),
        check_vma=False,
    )
```

```python
import math

import jax
import jax.numpy as jnp
from jax import lax
from jax.experimental import pallas as pl
from jax.experimental.pallas import tpu as pltpu
from jax.sharding import PartitionSpec as P

F32 = jnp.float32
BF16 = jnp.bfloat16
MESH = pl.DeviceIdType.MESH

NOPE = 128
ROPE = 64
LAT = 512
CAP = 8
N_CTX = 32
KW = LAT + 2 * ROPE
RUN = 64
PIECE = 32
GROUP = 256
BLOCK = 512
SCALE = 1.0 / math.sqrt(NOPE + ROPE)
LOG2E = math.log2(math.e)
LOW = -1e30


def dot(a, b):
    return jnp.dot(a, b, preferred_element_type=F32)


def dot_t(a, b):
    return lax.dot_general(a, b, (((1,), (1,)), ((), ())), preferred_element_type=F32)


def dot_0(a, b):
    return lax.dot_general(a, b, (((0,), (0,)), ((), ())), preferred_element_type=F32)


def iota(shape, dim):
    return lax.broadcasted_iota(jnp.int32, shape, dim)


def kernel(
    positions_h,
    latent_h,
    k_rope_h,
    rows_h,
    ids_h,
    weights_h,
    q_nope_h,
    q_rope_h,
    w_uk_h,
    w_uv_h,
    w_gate_h,
    w_up_h,
    w_down_h,
    attn_out,
    moe_out,
    positions,
    latent,
    k_rope,
    rows,
    ids,
    weights,
    q_nope,
    q_rope,
    w_uk,
    w_gate,
    w_up,
    w_down,
    index_row,
    meta,
    outgoing,
    slots,
    to_mate,
    from_mate,
    to_pair,
    kept,
    from_pair,
    returned,
    keys,
    key_group,
    value_group,
    queries,
    acc,
    row_max,
    row_sum,
    mixed,
    load_sem,
    disp_send,
    disp_recv,
    pair_send,
    pair_recv,
    core_send,
    core_recv,
    ag_send,
    ag_recv,
    back_core_send,
    back_core_recv,
    back_pair_send,
    back_pair_recv,
    back_send,
    back_recv,
):
    ctx = lax.axis_index("ctx")
    ep = lax.axis_index("ep")
    h = ctx // 16
    z = (ctx // 4) % 4
    y = ctx % 4
    lo = ep // 2
    core = ep % 2
    ep_pair = (1 - lo) * 2 + core
    ep_mate = lo * 2 + (1 - core)
    part = rows.shape[1]
    half = part // 2

    def context(step, dz, dy):
        other = h if step == 0 else 1 - h
        return other * 16 + ((z + dz) % 4) * 4 + (y + dy) % 4

    def partner_ep(step):
        return ep if step == 0 else ep_pair

    def window(step):
        return (h if step == 0 else 1 - h) * 16

    def kept_lo(step):
        return lo if step == 0 else 1 - lo

    order = [(s, dz, dy) for s in range(2) for dz in (0, 1, 3, 2) for dy in (0, 1, 3, 2)]

    loads = [
        pltpu.make_async_copy(src, dst, load_sem.at[i])
        for i, (src, dst) in enumerate(
            (
                (ids_h, ids),
                (weights_h, weights),
                (rows_h, rows),
                (k_rope_h, k_rope),
                (latent_h, latent),
                (positions_h, positions),
                (q_nope_h, q_nope),
                (q_rope_h, q_rope),
                (w_uk_h, w_uk),
                (w_gate_h.at[0], w_gate),
                (w_up_h.at[0], w_up),
                (w_down_h.at[0], w_down),
            )
        )
    ]
    for load in loads[:9]:
        load.start()

    barrier = pltpu.get_barrier_semaphore()
    for s, dz, dy in order[1:]:
        pl.semaphore_signal(
            barrier, inc=1, device_id=(context(s, dz, dy), partner_ep(s)), device_id_type=MESH
        )
    pl.semaphore_signal(barrier, inc=1, device_id=(ctx, ep_pair), device_id_type=MESH)
    pl.semaphore_signal(barrier, inc=1, device_id=(ctx, ep_mate), device_id_type=MESH)

    for load in loads[:3]:
        load.wait()
    expert = iota((128, 128), 0)
    named = jnp.zeros((128, 128), F32)
    slot_weight = jnp.zeros((128, 128), F32)
    for k in range(ids.shape[0]):
        hit = (ids[k : k + 1, :] == expert) & (expert < N_CTX)
        named = jnp.where(hit, 1.0, named)
        slot_weight = jnp.where(hit, weights[k : k + 1, :], slot_weight)
    earlier = jnp.where(expert < iota((128, 128), 1), 1.0, 0.0).astype(BF16)
    named_b = named.astype(BF16)
    rank_b = dot(named_b, earlier).astype(BF16)
    spread = jnp.where(iota((256, 128), 0) // CAP == iota((256, 128), 1), 1.0, 0.0).astype(BF16)
    picked = (dot(spread, named_b) > 0.5) & (
        dot(spread, rank_b) == (iota((256, 128), 0) % CAP).astype(F32)
    )
    pick = jnp.where(picked, 1.0, 0.0).astype(BF16)
    for c in range(4):
        lhs = pick[64 * c : 64 * (c + 1)]
        first = dot(lhs, rows[:, :half]).reshape(8, CAP, half)
        second = dot(lhs, rows[:, half:]).reshape(8, CAP, half)
        outgoing[8 * c : 8 * (c + 1)] = jnp.concatenate([first, second], axis=1).astype(BF16)

    for load in loads[3:6]:
        load.wait()
    double = jnp.where(iota((ROPE, 128), 1) % ROPE == iota((ROPE, 128), 0), 1.0, 0.0).astype(BF16)
    majors, minors = (z, y), (y, z)
    own_place = [majors[f] * 4 + minors[f] for f in range(2)]
    rotated = dot_0(k_rope[...], double)
    rotated = jnp.where(core == 0, rotated[:RUN], rotated[RUN:]).astype(BF16)
    for f in range(2):
        own_rows = pl.ds(pl.multiple_of(core * RUN + f * PIECE, PIECE), PIECE)
        keys[core, f, h, own_place[f], :, :LAT] = latent[own_rows, :]
        keys[core, f, h, own_place[f], :, LAT:] = rotated[f * PIECE : (f + 1) * PIECE]

    pl.semaphore_wait(barrier, 33)

    own = pltpu.make_async_copy(outgoing.at[ctx], slots.at[ep, ctx], disp_recv.at[0, 0])
    own.start()
    for s, dz, dy in order[1:]:
        to = context(s, dz, dy)
        pltpu.make_async_remote_copy(
            src_ref=outgoing.at[to],
            dst_ref=slots.at[ep, ctx],
            send_sem=disp_send.at[0],
            recv_sem=disp_recv.at[s, dz],
            device_id=(to, partner_ep(s)),
            device_id_type=MESH,
        ).start()

    def at_axis(f, major_to, minor_to):
        return h * 16 + (major_to * 4 + minor_to if f == 0 else minor_to * 4 + major_to)

    def send_keys(region, sent, arrived, to):
        pltpu.make_async_remote_copy(
            src_ref=region,
            dst_ref=region,
            send_sem=ag_send.at[sent],
            recv_sem=ag_recv.at[arrived],
            device_id=to,
            device_id_type=MESH,
        ).start()

    def keys_first():
        for f in range(2):
            send_keys(keys.at[core, f, h, own_place[f]], 0, 0, ((1 - h) * 16 + z * 4 + y, ep_pair))

    def keys_second(which):
        side = h if which == 0 else 1 - h
        if which == 1:
            wait_for(keys.at[core, :, side, 0], ag_recv.at[0])
        for t in (1, 3, 2):
            for f in range(2):
                to = (at_axis(f, majors[f], (minors[f] + t) % 4), ep)
                send_keys(keys.at[core, f, side, own_place[f]], 1, 1 + which, to)

    def keys_third(which):
        side = h if which == 0 else 1 - h
        wait_for(keys.at[core, :, side, pl.ds(0, 3)], ag_recv.at[1 + which])
        for t in (1, 3, 2):
            for f in range(2):
                to = (at_axis(f, (majors[f] + t) % 4, minors[f]), ep)
                region = keys.at[core, f, side, pl.ds(majors[f] * 4, 4)]
                send_keys(region, 2, 2 + 3 * which + t, to)
        for f in range(2):
            region = keys.at[core, f, side, pl.ds(majors[f] * 4, 4)]
            send_keys(region, 3, 9, (ctx, ep_mate))

    def keys_share(which, t):
        side = h if which == 0 else 1 - h
        wait_for(keys.at[core, :, side, pl.ds(0, 4)], ag_recv.at[2 + 3 * which + t])
        for f in range(2):
            at = (majors[f] - t + 4) % 4
            send_keys(keys.at[core, f, side, pl.ds(at * 4, 4)], 3, 9, (ctx, ep_mate))

    def wait_for(ref, sem):
        pltpu.make_async_copy(ref, ref, sem).wait()

    keys_first()

    block = iota((N_CTX, 128), 0)
    held_0 = positions[:, 0:1] // RUN == iota((N_CTX, 128), 1)
    held_1 = positions[:, RUN : RUN + 1] // RUN == iota((N_CTX, 128), 1)
    where = jnp.sum(
        jnp.where(held_0, 2 * block, 0) + jnp.where(held_1, 2 * block + 1, 0), axis=0
    )
    index_row[...] = jnp.zeros(index_row.shape, jnp.int32)
    index_row[0:1, :] = where.reshape(1, 128)
    index_row[1:2, :] = positions[pl.ds(ctx, 1), :]
    index_copy = pltpu.make_async_copy(index_row, meta, load_sem.at[0])
    index_copy.start()

    for load in loads[6:9]:
        load.wait()
    for load in loads[9:]:
        load.start()
    unit = jnp.where(iota((128, 128), 0) == iota((128, 128), 1), 1.0, 0.0).astype(BF16)

    @pl.loop(0, 8)
    def _(pair):
        at = pl.ds(pl.multiple_of(pair * 128, 128), 128)
        cols = pl.ds(pl.multiple_of(pair * 256, 256), 256)
        for run in range(2):
            of_run = slice(run * RUN, (run + 1) * RUN)
            both = q_nope[of_run, cols].astype(F32)
            first = iota(both.shape, 1) < NOPE
            apart = jnp.concatenate(
                [jnp.where(first, both, 0.0), jnp.where(first, 0.0, both)], axis=0
            ).astype(BF16)
            queries[run, :LAT, at] = dot_t(w_uk[:, cols], apart).astype(BF16)
            both = q_rope[of_run, at].astype(F32)
            first = iota(both.shape, 1) < ROPE
            apart = jnp.concatenate(
                [jnp.where(first, both, 0.0), jnp.where(first, 0.0, both)], axis=0
            ).astype(BF16)
            queries[run, LAT:, at] = dot_t(unit, apart).astype(BF16)

    index_copy.wait()
    out_weights = pltpu.make_async_copy(w_uv_h, w_uk, load_sem.at[1])
    out_weights.start()

    def chunk(step, dz, lo_part):
        return slots.at[lo_part * 2 + core, pl.ds(window(step) + ((z - dz + 4) % 4) * 4, 4)]

    def relay(step, dz):
        region = chunk(step, dz, kept_lo(step))
        wait_for(region, disp_recv.at[step, dz])
        pltpu.make_async_remote_copy(
            src_ref=region,
            dst_ref=region,
            send_sem=pair_send.at[0],
            recv_sem=pair_recv.at[step, dz],
            device_id=(ctx, ep_pair),
            device_id_type=MESH,
        ).start()
        pltpu.make_async_remote_copy(
            src_ref=region,
            dst_ref=region,
            send_sem=core_send.at[0],
            recv_sem=core_recv.at[0, step],
            device_id=(ctx, ep_mate),
            device_id_type=MESH,
        ).start()

    def relay_again(step, dz):
        region = chunk(step, dz, 1 - kept_lo(step))
        wait_for(region, pair_recv.at[step, dz])
        pltpu.make_async_remote_copy(
            src_ref=region,
            dst_ref=region,
            send_sem=core_send.at[0],
            recv_sem=core_recv.at[1, step],
            device_id=(ctx, ep_mate),
            device_id_type=MESH,
        ).start()

    def from_experts(step):
        start = window(step)
        for j in range(2):
            lo_part = kept_lo(step) if j == 0 else 1 - kept_lo(step)
            wait_for(
                slots.at[lo_part * 2 + (1 - core), pl.ds(start, 16)], core_recv.at[j, step]
            )

        def some(p, carry):
            gate, up = carry
            taken = slots[p, pl.ds(start, 16)].astype(F32)
            for i in range(2):
                x = taken[:, CAP * i : CAP * (i + 1)].reshape(128, half).astype(BF16)
                at = pl.ds(pl.multiple_of(p * part + i * half, 128), half)
                gate = gate + dot(x, w_gate[at, :])
                up = up + dot(x, w_up[at, :])
            return gate, up

        width = w_gate.shape[1]
        gate, up = lax.fori_loop(
            0, 4, some, (jnp.zeros((128, width), F32), jnp.zeros((128, width), F32))
        )
        hidden = (gate / (1.0 + jnp.exp(-gate)) * up).astype(BF16)

        def through_down(p):
            both = []
            for i in range(2):
                at = pl.ds(pl.multiple_of(p * part + i * half, 128), half)
                both.append(dot(hidden, w_down[:, at]).reshape(16, CAP, half))
            return jnp.concatenate(both, axis=1)

        for j in range(2):
            lo_part = 1 - kept_lo(step) if j == 0 else kept_lo(step)
            to_mate[step, j] = through_down(lo_part * 2 + (1 - core)).astype(BF16)
            pltpu.make_async_remote_copy(
                src_ref=to_mate.at[step, j],
                dst_ref=from_mate.at[step, j],
                send_sem=back_core_send.at[step, j],
                recv_sem=back_core_recv.at[step, j],
                device_id=(ctx, ep_mate),
                device_id_type=MESH,
            ).start()
        mine = through_down((1 - kept_lo(step)) * 2 + core)
        wait_for(from_mate.at[step, 0], back_core_recv.at[step, 0])
        to_pair[step] = (mine + from_mate[step, 0].astype(F32)).astype(BF16)
        for dz in (0, 1, 3, 2):
            some_of = pl.ds(((z + dz) % 4) * 4, 4)
            pltpu.make_async_remote_copy(
                src_ref=to_pair.at[step, some_of],
                dst_ref=from_pair.at[step, some_of],
                send_sem=back_pair_send.at[step],
                recv_sem=back_pair_recv.at[step, dz],
                device_id=(ctx, ep_pair),
                device_id_type=MESH,
            ).start()
        mine = through_down(kept_lo(step) * 2 + core)
        wait_for(from_mate.at[step, 1], back_core_recv.at[step, 1])
        kept[step] = (mine + from_mate[step, 1].astype(F32)).astype(BF16)

    def send_back(step, dz):
        start = ((z + dz) % 4) * 4
        some_of = pl.ds(start, 4)
        wait_for(from_pair.at[step, some_of], back_pair_recv.at[step, dz])
        base = window(step) + start
        outgoing[pl.ds(base, 4)] = (
            kept[step, some_of].astype(F32) + from_pair[step, some_of].astype(F32)
        ).astype(BF16)
        for dy in (0, 1, 3, 2):
            to = base + (y + dy) % 4

            def send(to=to):
                pltpu.make_async_remote_copy(
                    src_ref=outgoing.at[to],
                    dst_ref=returned.at[ctx],
                    send_sem=back_send.at[0],
                    recv_sem=back_recv.at[step],
                    device_id=(to, partner_ep(step)),
                    device_id_type=MESH,
                ).start()

            if step == 0 and dy == 0:
                pl.when(dz != 0)(send)

                @pl.when(dz == 0)
                def _():
                    pltpu.make_async_copy(
                        outgoing.at[ctx], returned.at[ctx], back_recv.at[0]
                    ).start()

            else:
                send()

    run_0 = meta[1, 0] // RUN
    run_1 = meta[1, RUN] // RUN
    run_late = jnp.maximum(run_0, run_1)
    run_early = jnp.minimum(run_0, run_1)
    late_half = jnp.where(run_1 > run_0, 1, 0)
    late_steps = run_late // 4 + 1
    columns = queries.shape[2]

    def take_keys(group, count):
        for t in range(count // RUN):
            at = jnp.clip(meta[0, group * 4 + t], 0, 2 * N_CTX - 1)
            of, c = at % 2, at // 2
            z_at, y_at = (c // 4) % 4, c % 4
            first, second = t * RUN, t * RUN + PIECE
            key_group[first:second, :] = keys[of, 0, c // 16, z_at * 4 + y_at]
            key_group[second : second + PIECE, :] = keys[of, 1, c // 16, y_at * 4 + z_at]
        for t in range(count // 128):
            at = slice(t * 128, (t + 1) * 128)
            value_group[:, at] = key_group[at, :LAT].T

    def attend(i, wide):
        if wide:
            count, group, q_half = 2 * GROUP, 2 * i, late_half
        else:
            is_late = i < late_steps
            count = GROUP
            group = jnp.where(is_late, i, i - late_steps)
            q_half = jnp.where(is_late, late_half, 1 - late_half)
            q_run = jnp.where(is_late, run_late, run_early)
            turn = i == late_steps
        take_keys(group, count)

        def scores_of(b):
            scores = dot(
                key_group[:count, :], queries[q_half, :, b * BLOCK : (b + 1) * BLOCK]
            )
            if not wide:
                key_pos = group * GROUP + iota(scores.shape, 0)
                query_pos = q_run * RUN + iota(scores.shape, 1) % RUN
                scores = jnp.where(key_pos <= query_pos, scores, LOW)
            return scores

        following = scores_of(0)
        for b in range(columns // BLOCK):
            at = slice(b * BLOCK, (b + 1) * BLOCK)
            scores = following
            if (b + 1) * BLOCK < columns:
                following = scores_of(b + 1)
            old_max = row_max[:, at]
            if not wide:
                old_max = jnp.where(turn, LOW, old_max)
            new_max = jnp.maximum(old_max, jnp.max(scores, axis=0, keepdims=True))
            fade = jnp.exp2((old_max - new_max) * (SCALE * LOG2E))
            probs = jnp.exp2((scores - new_max[:1]) * (SCALE * LOG2E))
            new_sum = row_sum[:, at] * fade + jnp.sum(
                probs.reshape(count // 8, 8, BLOCK), axis=0
            )
            new_acc = acc[:, at] * fade[:1] + dot(value_group[:, :count], probs.astype(BF16))
            row_max[:, at] = new_max
            row_sum[:, at] = new_sum
            acc[:, at] = new_acc
            if not wide:
                whole = jnp.sum(new_sum, axis=0, keepdims=True)
                mixed[i - 8, :, at] = (new_acc * (1.0 / whole)).astype(BF16)

    row_max[...] = jnp.full(row_max.shape, LOW, F32)
    row_sum[...] = jnp.zeros(row_sum.shape, F32)
    acc[...] = jnp.zeros(acc.shape, F32)

    def gray(i):
        return jnp.where(i < 2, i, 5 - i)

    relay(0, 0)
    keys_second(0)
    relay(0, 1)
    keys_second(1)
    relay(0, 3)
    relay(0, 2)
    relay(1, 0)
    keys_third(0)
    relay(1, 1)
    keys_third(1)
    relay(1, 3)
    relay(1, 2)
    relay_again(0, 0)
    relay_again(0, 1)
    relay_again(0, 3)
    relay_again(0, 2)
    for load in loads[9:]:
        load.wait()
    wait_for(outgoing.at[pl.ds(0, 31)], disp_send.at[0])
    from_experts(0)
    keys_share(0, 1)
    relay_again(1, 0)
    keys_share(0, 3)
    relay_again(1, 1)
    keys_share(0, 2)
    relay_again(1, 3)
    relay_again(1, 2)
    from_experts(1)
    keys_share(1, 1)
    keys_share(1, 3)
    keys_share(1, 2)
    wait_for(keys.at[1 - core], ag_recv.at[9])

    @pl.loop(0, 4)
    def _(i):
        attend(i, True)
        send_back(0, gray(i))

    @pl.loop(0, 4)
    def _(i):
        attend(8 + 2 * i, False)
        attend(9 + 2 * i, False)
        send_back(1, gray(i))

    attend(jnp.int32(16), False)

    out_weights.wait()
    late_at = jnp.clip(late_steps - 9, 0, 7)

    @pl.loop(0, 8)
    def _(pair):
        at = pl.ds(pl.multiple_of(pair * 128, 128), 128)
        for run in range(2):
            place = jnp.where(late_half == run, late_at, 8)
            cols = pl.ds(pl.multiple_of(pair * 256, 256), 256)
            both = dot_0(mixed[place, :, at], w_uk[:, cols])
            for i in range(2):
                to = pl.ds(pl.multiple_of(pair * 256 + i * 128, 128), 128)
                attn_out[run * RUN : (run + 1) * RUN, to] = both[
                    i * RUN : (i + 1) * RUN, i * 128 : (i + 1) * 128
                ].astype(BF16)

    wide = (128, N_CTX * 2 * CAP)
    column = iota(wide, 1)
    spread_2 = jnp.where(column // (2 * CAP) == iota(wide, 0), 1.0, 0.0).astype(BF16)
    weight_hi = slot_weight.astype(BF16)
    weight_lo = (slot_weight - weight_hi.astype(F32)).astype(BF16)
    here = (dot_0(named_b, spread_2) > 0.5) & (
        dot_0(rank_b, spread_2) == (column % CAP).astype(F32)
    )
    parts = [dot_0(w, spread_2) for w in (weight_hi, weight_lo)]
    wait_for(returned.at[pl.ds(0, 16)], back_recv.at[0])
    wait_for(returned.at[pl.ds(0, 16)], back_recv.at[1])
    for i in range(2):
        mine = here & ((column // CAP) % 2 == i)
        total = jnp.zeros((128, half), F32)
        for w in parts:
            factor = jnp.where(mine, w, 0.0).astype(BF16)
            total = total + dot(factor, returned[...].reshape(N_CTX * 2 * CAP, half))
        moe_out[:, i * half : (i + 1) * half] = total.astype(BF16)

    wait_for(slots.at[0], pair_send.at[0])
    wait_for(slots.at[pl.ds(0, 2)], core_send.at[0])
    wait_for(keys.at[0, :, 0, 0], ag_send.at[0])
    wait_for(keys.at[0, 0, 0, pl.ds(0, 12)], ag_send.at[1])
    wait_for(keys.at[0, :, :, pl.ds(0, 12)], ag_send.at[2])
    wait_for(keys.at[0], ag_send.at[3])
    for step in range(2):
        for j in range(2):
            wait_for(to_mate.at[step, j], back_core_send.at[step, j])
        wait_for(to_pair.at[step], back_pair_send.at[step])
    wait_for(outgoing.at[pl.ds(0, 31)], back_send.at[0])


def shards(
    q_nope,
    q_rope,
    latent,
    k_rope,
    w_uk,
    w_uv,
    positions,
    moe_rows,
    expert_ids,
    expert_weights,
    w_gate,
    w_up,
    w_down,
):
    count, part = moe_rows.shape
    half = part // 2
    vmem = pl.BlockSpec(memory_space=pltpu.VMEM)
    anywhere = pl.BlockSpec(memory_space=pl.ANY)
    dma = pltpu.SemaphoreType.DMA
    columns = q_nope.shape[1] // NOPE * RUN
    slot = (2 * CAP, half)
    return pl.pallas_call(
        kernel,
        out_shape=(
            jax.ShapeDtypeStruct(q_nope.shape, BF16),
            jax.ShapeDtypeStruct(moe_rows.shape, BF16),
        ),
        in_specs=[anywhere] * 13,
        out_specs=(vmem, vmem),
        scratch_shapes=[
            pltpu.VMEM((N_CTX, count), jnp.int32),
            pltpu.VMEM(latent.shape, BF16),
            pltpu.VMEM(k_rope.shape[::-1], BF16),
            pltpu.VMEM(moe_rows.shape, BF16),
            pltpu.VMEM(expert_ids.shape[::-1], jnp.int32),
            pltpu.VMEM(expert_weights.shape[::-1], F32),
            pltpu.VMEM(q_nope.shape, BF16),
            pltpu.VMEM(q_rope.shape, BF16),
            pltpu.VMEM(w_uk.shape, BF16),
            pltpu.VMEM(w_gate.shape[1:], BF16),
            pltpu.VMEM(w_up.shape[1:], BF16),
            pltpu.VMEM(w_down.shape[1:], BF16),
            pltpu.VMEM((8, 128), jnp.int32),
            pltpu.SMEM((8, 128), jnp.int32),
            pltpu.VMEM((N_CTX,) + slot, BF16),
            pltpu.VMEM((4, N_CTX) + slot, BF16),
            pltpu.VMEM((2, 2, 16) + slot, BF16),
            pltpu.VMEM((2, 2, 16) + slot, BF16),
            pltpu.VMEM((2, 16) + slot, BF16),
            pltpu.VMEM((2, 16) + slot, BF16),
            pltpu.VMEM((2, 16) + slot, BF16),
            pltpu.VMEM((N_CTX,) + slot, BF16),
            pltpu.VMEM((2, 2, 2, 16, PIECE, KW), BF16),
            pltpu.VMEM((2 * GROUP, KW), BF16),
            pltpu.VMEM((LAT, 2 * GROUP), BF16),
            pltpu.VMEM((2, KW, columns), BF16),
            pltpu.VMEM((LAT, columns), F32),
            pltpu.VMEM((8, columns), F32),
            pltpu.VMEM((8, columns), F32),
            pltpu.VMEM((9, LAT, columns), BF16),
            dma((12,)),
            dma((1,)),
            dma((2, 4)),
            dma((1,)),
            dma((2, 4)),
            dma((1,)),
            dma((2, 2)),
            dma((4,)),
            dma((10,)),
            dma((2, 2)),
            dma((2, 2)),
            dma((2,)),
            dma((2, 4)),
            dma((1,)),
            dma((2,)),
        ],
        compiler_params=pltpu.CompilerParams(
            collective_id=0, has_side_effects=True, vmem_limit_bytes=56 * 1024 * 1024
        ),
        name="attend_and_dispatch",
    )(
        positions.reshape(N_CTX, count),
        latent,
        k_rope.T,
        moe_rows,
        expert_ids.T,
        expert_weights.T,
        q_nope,
        q_rope,
        w_uk,
        w_uv,
        w_gate,
        w_up,
        w_down,
    )


def solution(mesh):
    return jax.shard_map(
        shards,
        mesh=mesh,
        in_specs=(
            P("ctx", "ep"),
            P("ctx", "ep"),
            P("ctx", None),
            P("ctx", None),
            P(None, "ep"),
            P(None, "ep"),
            P(),
            P("ctx", "ep"),
            P("ctx", None),
            P("ctx", None),
            P("ctx", None, "ep"),
            P("ctx", None, "ep"),
            P("ctx", "ep", None),
        ),
        out_specs=(P("ctx", "ep"), P("ctx", "ep")),
        check_vma=False,
    )
```

```python
import math

import jax
import jax.numpy as jnp
from jax import lax
from jax.experimental import pallas as pl
from jax.experimental.pallas import tpu as pltpu
from jax.sharding import PartitionSpec as P

F32 = jnp.float32
BF16 = jnp.bfloat16
MESH = pl.DeviceIdType.MESH

NOPE = 128
ROPE = 64
LAT = 512
CAP = 8
N_CTX = 32
KW = LAT + 2 * ROPE
RUN = 64
PIECE = 32
GROUP = 256
BLOCK = 512
SCALE = 1.0 / math.sqrt(NOPE + ROPE)
LOG2E = math.log2(math.e)
LOW = -1e30


def dot(a, b):
    return jnp.dot(a, b, preferred_element_type=F32)


def dot_t(a, b):
    return lax.dot_general(a, b, (((1,), (1,)), ((), ())), preferred_element_type=F32)


def dot_0(a, b):
    return lax.dot_general(a, b, (((0,), (0,)), ((), ())), preferred_element_type=F32)


def iota(shape, dim):
    return lax.broadcasted_iota(jnp.int32, shape, dim)


def kernel(
    positions_h,
    latent_h,
    k_rope_h,
    rows_h,
    ids_h,
    weights_h,
    q_nope_h,
    q_rope_h,
    w_uk_h,
    w_uv_h,
    w_gate_h,
    w_up_h,
    w_down_h,
    attn_out,
    moe_out,
    positions,
    latent,
    k_rope,
    rows,
    ids,
    weights,
    q_nope,
    q_rope,
    w_uk,
    w_gate,
    w_up,
    w_down,
    index_row,
    meta,
    outgoing,
    slots,
    to_mate,
    from_mate,
    to_pair,
    kept,
    from_pair,
    returned,
    keys,
    key_group,
    value_group,
    queries,
    acc,
    row_max,
    row_sum,
    mixed,
    load_sem,
    disp_send,
    disp_recv,
    pair_send,
    pair_recv,
    core_send,
    core_recv,
    ag_send,
    ag_recv,
    back_core_send,
    back_core_recv,
    back_pair_send,
    back_pair_recv,
    back_send,
    back_recv,
):
    ctx = lax.axis_index("ctx")
    ep = lax.axis_index("ep")
    h = ctx // 16
    z = (ctx // 4) % 4
    y = ctx % 4
    lo = ep // 2
    core = ep % 2
    ep_pair = (1 - lo) * 2 + core
    ep_mate = lo * 2 + (1 - core)
    part = rows.shape[1]
    half = part // 2

    def context(step, dz, dy):
        other = h if step == 0 else 1 - h
        return other * 16 + ((z + dz) % 4) * 4 + (y + dy) % 4

    def partner_ep(step):
        return ep if step == 0 else ep_pair

    def window(step):
        return (h if step == 0 else 1 - h) * 16

    def kept_lo(step):
        return lo if step == 0 else 1 - lo

    order = [(s, dz, dy) for s in range(2) for dz in (0, 1, 3, 2) for dy in (0, 1, 3, 2)]

    loads = [
        pltpu.make_async_copy(src, dst, load_sem.at[i])
        for i, (src, dst) in enumerate(
            (
                (ids_h, ids),
                (weights_h, weights),
                (rows_h, rows),
                (k_rope_h, k_rope),
                (latent_h, latent),
                (positions_h, positions),
                (q_nope_h, q_nope),
                (q_rope_h, q_rope),
                (w_uk_h, w_uk),
                (w_gate_h.at[0], w_gate),
                (w_up_h.at[0], w_up),
                (w_down_h.at[0], w_down),
            )
        )
    ]
    for load in loads[:9]:
        load.start()

    barrier = pltpu.get_barrier_semaphore()
    for s, dz, dy in order[1:]:
        pl.semaphore_signal(
            barrier, inc=1, device_id=(context(s, dz, dy), partner_ep(s)), device_id_type=MESH
        )
    pl.semaphore_signal(barrier, inc=1, device_id=(ctx, ep_pair), device_id_type=MESH)
    pl.semaphore_signal(barrier, inc=1, device_id=(ctx, ep_mate), device_id_type=MESH)

    for load in loads[:3]:
        load.wait()
    expert = iota((128, 128), 0)
    named = jnp.zeros((128, 128), F32)
    slot_weight = jnp.zeros((128, 128), F32)
    for k in range(ids.shape[0]):
        hit = (ids[k : k + 1, :] == expert) & (expert < N_CTX)
        named = jnp.where(hit, 1.0, named)
        slot_weight = jnp.where(hit, weights[k : k + 1, :], slot_weight)
    earlier = jnp.where(expert < iota((128, 128), 1), 1.0, 0.0).astype(BF16)
    named_b = named.astype(BF16)
    rank_b = dot(named_b, earlier).astype(BF16)
    spread = jnp.where(iota((256, 128), 0) // CAP == iota((256, 128), 1), 1.0, 0.0).astype(BF16)
    picked = (dot(spread, named_b) > 0.5) & (
        dot(spread, rank_b) == (iota((256, 128), 0) % CAP).astype(F32)
    )
    pick = jnp.where(picked, 1.0, 0.0).astype(BF16)
    for c in range(4):
        lhs = pick[64 * c : 64 * (c + 1)]
        first = dot(lhs, rows[:, :half]).reshape(8, CAP, half)
        second = dot(lhs, rows[:, half:]).reshape(8, CAP, half)
        outgoing[8 * c : 8 * (c + 1)] = jnp.concatenate([first, second], axis=1).astype(BF16)

    for load in loads[3:6]:
        load.wait()
    double = jnp.where(iota((ROPE, 128), 1) % ROPE == iota((ROPE, 128), 0), 1.0, 0.0).astype(BF16)
    majors, minors = (z, y), (y, z)
    own_place = [majors[f] * 4 + minors[f] for f in range(2)]
    rotated = dot_0(k_rope[...], double)
    rotated = jnp.where(core == 0, rotated[:RUN], rotated[RUN:]).astype(BF16)
    for f in range(2):
        own_rows = pl.ds(pl.multiple_of(core * RUN + f * PIECE, PIECE), PIECE)
        keys[core, f, h, own_place[f], :, :LAT] = latent[own_rows, :]
        keys[core, f, h, own_place[f], :, LAT:] = rotated[f * PIECE : (f + 1) * PIECE]

    pl.semaphore_wait(barrier, 33)

    own = pltpu.make_async_copy(outgoing.at[ctx], slots.at[ep, ctx], disp_recv.at[0, 0])
    own.start()
    for s, dz, dy in order[1:]:
        to = context(s, dz, dy)
        pltpu.make_async_remote_copy(
            src_ref=outgoing.at[to],
            dst_ref=slots.at[ep, ctx],
            send_sem=disp_send.at[0],
            recv_sem=disp_recv.at[s, dz],
            device_id=(to, partner_ep(s)),
            device_id_type=MESH,
        ).start()

    def at_axis(f, major_to, minor_to):
        return h * 16 + (major_to * 4 + minor_to if f == 0 else minor_to * 4 + major_to)

    def send_keys(region, sent, arrived, to):
        pltpu.make_async_remote_copy(
            src_ref=region,
            dst_ref=region,
            send_sem=ag_send.at[sent],
            recv_sem=ag_recv.at[arrived],
            device_id=to,
            device_id_type=MESH,
        ).start()

    def keys_first():
        for f in range(2):
            send_keys(keys.at[core, f, h, own_place[f]], 0, 0, ((1 - h) * 16 + z * 4 + y, ep_pair))

    def keys_second(which):
        side = h if which == 0 else 1 - h
        if which == 1:
            wait_for(keys.at[core, :, side, 0], ag_recv.at[0])
        for t in (1, 3, 2):
            for f in range(2):
                to = (at_axis(f, majors[f], (minors[f] + t) % 4), ep)
                send_keys(keys.at[core, f, side, own_place[f]], 1, 1 + which, to)

    def keys_third(which):
        side = h if which == 0 else 1 - h
        wait_for(keys.at[core, :, side, pl.ds(0, 3)], ag_recv.at[1 + which])
        for t in (1, 3, 2):
            for f in range(2):
                to = (at_axis(f, (majors[f] + t) % 4, minors[f]), ep)
                region = keys.at[core, f, side, pl.ds(majors[f] * 4, 4)]
                send_keys(region, 2, 2 + 3 * which + t, to)
        for f in range(2):
            region = keys.at[core, f, side, pl.ds(majors[f] * 4, 4)]
            send_keys(region, 3, 9, (ctx, ep_mate))

    def keys_share(which, t):
        side = h if which == 0 else 1 - h
        wait_for(keys.at[core, :, side, pl.ds(0, 4)], ag_recv.at[2 + 3 * which + t])
        for f in range(2):
            at = (majors[f] - t + 4) % 4
            send_keys(keys.at[core, f, side, pl.ds(at * 4, 4)], 3, 9 + t, (ctx, ep_mate))

    def wait_for(ref, sem):
        pltpu.make_async_copy(ref, ref, sem).wait()

    keys_first()

    block = iota((N_CTX, 128), 0)
    held_0 = positions[:, 0:1] // RUN == iota((N_CTX, 128), 1)
    held_1 = positions[:, RUN : RUN + 1] // RUN == iota((N_CTX, 128), 1)
    where = jnp.sum(
        jnp.where(held_0, 2 * block, 0) + jnp.where(held_1, 2 * block + 1, 0), axis=0
    )
    index_row[...] = jnp.zeros(index_row.shape, jnp.int32)
    index_row[0:1, :] = where.reshape(1, 128)
    index_row[1:2, :] = positions[pl.ds(ctx, 1), :]
    swapped = jnp.where(positions[:, 0:1] > positions[:, RUN : RUN + 1], 1, 0)
    swapped = jnp.sum(jnp.where(block == iota((N_CTX, 128), 1), swapped, 0), axis=0)
    index_row[2:3, :] = swapped.reshape(1, 128)
    index_copy = pltpu.make_async_copy(index_row, meta, load_sem.at[0])
    index_copy.start()

    for load in loads[6:9]:
        load.wait()
    for load in loads[9:]:
        load.start()
    unit = jnp.where(iota((128, 128), 0) == iota((128, 128), 1), 1.0, 0.0).astype(BF16)

    @pl.loop(0, 8)
    def _(pair):
        at = pl.ds(pl.multiple_of(pair * 128, 128), 128)
        cols = pl.ds(pl.multiple_of(pair * 256, 256), 256)
        for run in range(2):
            of_run = slice(run * RUN, (run + 1) * RUN)
            both = q_nope[of_run, cols].astype(F32)
            first = iota(both.shape, 1) < NOPE
            apart = jnp.concatenate(
                [jnp.where(first, both, 0.0), jnp.where(first, 0.0, both)], axis=0
            ).astype(BF16)
            queries[run, :LAT, at] = dot_t(w_uk[:, cols], apart).astype(BF16)
            both = q_rope[of_run, at].astype(F32)
            first = iota(both.shape, 1) < ROPE
            apart = jnp.concatenate(
                [jnp.where(first, both, 0.0), jnp.where(first, 0.0, both)], axis=0
            ).astype(BF16)
            queries[run, LAT:, at] = dot_t(unit, apart).astype(BF16)

    index_copy.wait()
    out_weights = pltpu.make_async_copy(w_uv_h, w_uk, load_sem.at[1])
    out_weights.start()

    def chunk(step, dz, lo_part):
        return slots.at[lo_part * 2 + core, pl.ds(window(step) + ((z - dz + 4) % 4) * 4, 4)]

    def relay(step, dz):
        region = chunk(step, dz, kept_lo(step))
        wait_for(region, disp_recv.at[step, dz])
        pltpu.make_async_remote_copy(
            src_ref=region,
            dst_ref=region,
            send_sem=pair_send.at[0],
            recv_sem=pair_recv.at[step, dz],
            device_id=(ctx, ep_pair),
            device_id_type=MESH,
        ).start()
        pltpu.make_async_remote_copy(
            src_ref=region,
            dst_ref=region,
            send_sem=core_send.at[0],
            recv_sem=core_recv.at[0, step],
            device_id=(ctx, ep_mate),
            device_id_type=MESH,
        ).start()

    def relay_again(step, dz):
        region = chunk(step, dz, 1 - kept_lo(step))
        wait_for(region, pair_recv.at[step, dz])
        pltpu.make_async_remote_copy(
            src_ref=region,
            dst_ref=region,
            send_sem=core_send.at[0],
            recv_sem=core_recv.at[1, step],
            device_id=(ctx, ep_mate),
            device_id_type=MESH,
        ).start()

    def from_experts(step):
        start = window(step)
        for j in range(2):
            lo_part = kept_lo(step) if j == 0 else 1 - kept_lo(step)
            wait_for(
                slots.at[lo_part * 2 + (1 - core), pl.ds(start, 16)], core_recv.at[j, step]
            )

        def some(p, carry):
            gate, up = carry
            taken = slots[p, pl.ds(start, 16)].astype(F32)
            for i in range(2):
                x = taken[:, CAP * i : CAP * (i + 1)].reshape(128, half).astype(BF16)
                at = pl.ds(pl.multiple_of(p * part + i * half, 128), half)
                gate = gate + dot(x, w_gate[at, :])
                up = up + dot(x, w_up[at, :])
            return gate, up

        width = w_gate.shape[1]
        gate, up = lax.fori_loop(
            0, 4, some, (jnp.zeros((128, width), F32), jnp.zeros((128, width), F32))
        )
        hidden = (gate / (1.0 + jnp.exp(-gate)) * up).astype(BF16)

        def through_down(p):
            both = []
            for i in range(2):
                at = pl.ds(pl.multiple_of(p * part + i * half, 128), half)
                both.append(dot(hidden, w_down[:, at]).reshape(16, CAP, half))
            return jnp.concatenate(both, axis=1)

        for j in range(2):
            lo_part = 1 - kept_lo(step) if j == 0 else kept_lo(step)
            to_mate[step, j] = through_down(lo_part * 2 + (1 - core)).astype(BF16)
            pltpu.make_async_remote_copy(
                src_ref=to_mate.at[step, j],
                dst_ref=from_mate.at[step, j],
                send_sem=back_core_send.at[step, j],
                recv_sem=back_core_recv.at[step, j],
                device_id=(ctx, ep_mate),
                device_id_type=MESH,
            ).start()
        mine = through_down((1 - kept_lo(step)) * 2 + core)
        wait_for(from_mate.at[step, 0], back_core_recv.at[step, 0])
        to_pair[step] = (mine + from_mate[step, 0].astype(F32)).astype(BF16)
        for dz in (0, 1, 3, 2):
            some_of = pl.ds(((z + dz) % 4) * 4, 4)
            pltpu.make_async_remote_copy(
                src_ref=to_pair.at[step, some_of],
                dst_ref=from_pair.at[step, some_of],
                send_sem=back_pair_send.at[step],
                recv_sem=back_pair_recv.at[step, dz],
                device_id=(ctx, ep_pair),
                device_id_type=MESH,
            ).start()
        mine = through_down(kept_lo(step) * 2 + core)
        wait_for(from_mate.at[step, 1], back_core_recv.at[step, 1])
        kept[step] = (mine + from_mate[step, 1].astype(F32)).astype(BF16)

    def send_back(step, dz):
        start = ((z + dz) % 4) * 4
        some_of = pl.ds(start, 4)
        wait_for(from_pair.at[step, some_of], back_pair_recv.at[step, dz])
        base = window(step) + start
        outgoing[pl.ds(base, 4)] = (
            kept[step, some_of].astype(F32) + from_pair[step, some_of].astype(F32)
        ).astype(BF16)
        for dy in (0, 1, 3, 2):
            to = base + (y + dy) % 4

            def send(to=to):
                pltpu.make_async_remote_copy(
                    src_ref=outgoing.at[to],
                    dst_ref=returned.at[ctx],
                    send_sem=back_send.at[0],
                    recv_sem=back_recv.at[step],
                    device_id=(to, partner_ep(step)),
                    device_id_type=MESH,
                ).start()

            if step == 0 and dy == 0:
                pl.when(dz != 0)(send)

                @pl.when(dz == 0)
                def _():
                    pltpu.make_async_copy(
                        outgoing.at[ctx], returned.at[ctx], back_recv.at[0]
                    ).start()

            else:
                send()

    run_0 = meta[1, 0] // RUN
    run_1 = meta[1, RUN] // RUN
    run_late = jnp.maximum(run_0, run_1)
    run_early = jnp.minimum(run_0, run_1)
    late_half = jnp.where(run_1 > run_0, 1, 0)
    late_steps = run_late // 4 + 1
    columns = queries.shape[2]

    def take_values(count):
        for t in range(count // 128):
            at = slice(t * 128, (t + 1) * 128)
            value_group[:, at] = key_group[at, :LAT].T

    def take_early(t):
        for f in range(2):
            row = (majors[f] - t + 4) % 4
            for n in range(8):
                side, a = n // 4, n % 4
                c = side * 16 + (row * 4 + a if f == 0 else a * 4 + row)
                to = (f * 8 + n) * PIECE
                key_group[to : to + PIECE, :] = jnp.where(
                    meta[2, c] == 1, keys[1, f, side, row * 4 + a], keys[0, f, side, row * 4 + a]
                )
        take_values(2 * GROUP)

    def take_keys(group, count):
        for t in range(count // RUN):
            at = jnp.clip(meta[0, group * 4 + t], 0, 2 * N_CTX - 1)
            of, c = at % 2, at // 2
            z_at, y_at = (c // 4) % 4, c % 4
            first, second = t * RUN, t * RUN + PIECE
            key_group[first:second, :] = keys[of, 0, c // 16, z_at * 4 + y_at]
            key_group[second : second + PIECE, :] = keys[of, 1, c // 16, y_at * 4 + z_at]
        take_values(count)

    def attend(i, wide):
        if wide:
            count, q_half = 2 * GROUP, late_half
            take_early(i)
        else:
            is_late = i < late_steps
            count = GROUP
            group = jnp.where(is_late, i, i - late_steps)
            q_half = jnp.where(is_late, late_half, 1 - late_half)
            q_run = jnp.where(is_late, run_late, run_early)
            turn = i == late_steps
            take_keys(group, count)

        def scores_of(b):
            scores = dot(
                key_group[:count, :], queries[q_half, :, b * BLOCK : (b + 1) * BLOCK]
            )
            if not wide:
                key_pos = group * GROUP + iota(scores.shape, 0)
                query_pos = q_run * RUN + iota(scores.shape, 1) % RUN
                scores = jnp.where(key_pos <= query_pos, scores, LOW)
            return scores

        following = scores_of(0)
        for b in range(columns // BLOCK):
            at = slice(b * BLOCK, (b + 1) * BLOCK)
            scores = following
            if (b + 1) * BLOCK < columns:
                following = scores_of(b + 1)
            old_max = row_max[:, at]
            if not wide:
                old_max = jnp.where(turn, LOW, old_max)
            new_max = jnp.maximum(old_max, jnp.max(scores, axis=0, keepdims=True))
            fade = jnp.exp2((old_max - new_max) * (SCALE * LOG2E))
            probs = jnp.exp2((scores - new_max[:1]) * (SCALE * LOG2E))
            new_sum = row_sum[:, at] * fade + jnp.sum(
                probs.reshape(count // 8, 8, BLOCK), axis=0
            )
            new_acc = acc[:, at] * fade[:1] + dot(value_group[:, :count], probs.astype(BF16))
            row_max[:, at] = new_max
            row_sum[:, at] = new_sum
            acc[:, at] = new_acc
            if not wide:
                whole = jnp.sum(new_sum, axis=0, keepdims=True)
                mixed[i - 8, :, at] = (new_acc * (1.0 / whole)).astype(BF16)

    row_max[...] = jnp.full(row_max.shape, LOW, F32)
    row_sum[...] = jnp.zeros(row_sum.shape, F32)
    acc[...] = jnp.zeros(acc.shape, F32)

    def gray(i):
        return jnp.where(i < 2, i, 5 - i)

    def attend_early(t):
        wait_for(keys.at[1 - core, :, :, pl.ds(0, 4)], ag_recv.at[9 + t])
        attend(t, True)

    relay(0, 0)
    keys_second(0)
    relay(0, 1)
    keys_second(1)
    relay(0, 3)
    relay(0, 2)
    relay(1, 0)
    keys_third(0)
    relay(1, 1)
    keys_third(1)
    relay(1, 3)
    relay(1, 2)
    relay_again(0, 0)
    relay_again(0, 1)
    relay_again(0, 3)
    relay_again(0, 2)
    for load in loads[9:]:
        load.wait()
    wait_for(outgoing.at[pl.ds(0, 31)], disp_send.at[0])
    from_experts(0)
    keys_share(0, 1)
    relay_again(1, 0)
    keys_share(0, 3)
    relay_again(1, 1)
    keys_share(0, 2)
    relay_again(1, 3)
    relay_again(1, 2)
    from_experts(1)
    keys_share(1, 1)
    attend_early(0)
    send_back(0, 0)
    keys_share(1, 3)
    attend_early(1)
    send_back(0, 1)
    keys_share(1, 2)
    attend_early(3)
    send_back(0, 3)
    attend_early(2)
    send_back(0, 2)

    @pl.loop(0, 4)
    def _(i):
        attend(8 + 2 * i, False)
        attend(9 + 2 * i, False)
        send_back(1, gray(i))

    attend(jnp.int32(16), False)

    out_weights.wait()
    late_at = jnp.clip(late_steps - 9, 0, 7)

    @pl.loop(0, 8)
    def _(pair):
        at = pl.ds(pl.multiple_of(pair * 128, 128), 128)
        for run in range(2):
            place = jnp.where(late_half == run, late_at, 8)
            cols = pl.ds(pl.multiple_of(pair * 256, 256), 256)
            both = dot_0(mixed[place, :, at], w_uk[:, cols])
            for i in range(2):
                to = pl.ds(pl.multiple_of(pair * 256 + i * 128, 128), 128)
                attn_out[run * RUN : (run + 1) * RUN, to] = both[
                    i * RUN : (i + 1) * RUN, i * 128 : (i + 1) * 128
                ].astype(BF16)

    wide = (128, N_CTX * 2 * CAP)
    column = iota(wide, 1)
    spread_2 = jnp.where(column // (2 * CAP) == iota(wide, 0), 1.0, 0.0).astype(BF16)
    weight_hi = slot_weight.astype(BF16)
    weight_lo = (slot_weight - weight_hi.astype(F32)).astype(BF16)
    here = (dot_0(named_b, spread_2) > 0.5) & (
        dot_0(rank_b, spread_2) == (column % CAP).astype(F32)
    )
    parts = [dot_0(w, spread_2) for w in (weight_hi, weight_lo)]
    wait_for(returned.at[pl.ds(0, 16)], back_recv.at[0])
    wait_for(returned.at[pl.ds(0, 16)], back_recv.at[1])
    for i in range(2):
        mine = here & ((column // CAP) % 2 == i)
        total = jnp.zeros((128, half), F32)
        for w in parts:
            factor = jnp.where(mine, w, 0.0).astype(BF16)
            total = total + dot(factor, returned[...].reshape(N_CTX * 2 * CAP, half))
        moe_out[:, i * half : (i + 1) * half] = total.astype(BF16)

    wait_for(slots.at[0], pair_send.at[0])
    wait_for(slots.at[pl.ds(0, 2)], core_send.at[0])
    wait_for(keys.at[0, :, 0, 0], ag_send.at[0])
    wait_for(keys.at[0, 0, 0, pl.ds(0, 12)], ag_send.at[1])
    wait_for(keys.at[0, :, :, pl.ds(0, 12)], ag_send.at[2])
    wait_for(keys.at[0], ag_send.at[3])
    for step in range(2):
        for j in range(2):
            wait_for(to_mate.at[step, j], back_core_send.at[step, j])
        wait_for(to_pair.at[step], back_pair_send.at[step])
    wait_for(outgoing.at[pl.ds(0, 31)], back_send.at[0])


def hand_over(attn, moe, attn_out, moe_out):
    attn_out[...] = attn[...]
    moe_out[...] = moe[...]


def shards(
    q_nope,
    q_rope,
    latent,
    k_rope,
    w_uk,
    w_uv,
    positions,
    moe_rows,
    expert_ids,
    expert_weights,
    w_gate,
    w_up,
    w_down,
):
    count, part = moe_rows.shape
    half = part // 2
    vmem = pl.BlockSpec(memory_space=pltpu.VMEM)
    anywhere = pl.BlockSpec(memory_space=pl.ANY)
    dma = pltpu.SemaphoreType.DMA
    columns = q_nope.shape[1] // NOPE * RUN
    slot = (2 * CAP, half)
    results = pl.pallas_call(
        kernel,
        out_shape=(
            jax.ShapeDtypeStruct(q_nope.shape, BF16),
            jax.ShapeDtypeStruct(moe_rows.shape, BF16),
        ),
        in_specs=[anywhere] * 13,
        out_specs=(vmem, vmem),
        scratch_shapes=[
            pltpu.VMEM((N_CTX, count), jnp.int32),
            pltpu.VMEM(latent.shape, BF16),
            pltpu.VMEM(k_rope.shape[::-1], BF16),
            pltpu.VMEM(moe_rows.shape, BF16),
            pltpu.VMEM(expert_ids.shape[::-1], jnp.int32),
            pltpu.VMEM(expert_weights.shape[::-1], F32),
            pltpu.VMEM(q_nope.shape, BF16),
            pltpu.VMEM(q_rope.shape, BF16),
            pltpu.VMEM(w_uk.shape, BF16),
            pltpu.VMEM(w_gate.shape[1:], BF16),
            pltpu.VMEM(w_up.shape[1:], BF16),
            pltpu.VMEM(w_down.shape[1:], BF16),
            pltpu.VMEM((8, 128), jnp.int32),
            pltpu.SMEM((8, 128), jnp.int32),
            pltpu.VMEM((N_CTX,) + slot, BF16),
            pltpu.VMEM((4, N_CTX) + slot, BF16),
            pltpu.VMEM((2, 2, 16) + slot, BF16),
            pltpu.VMEM((2, 2, 16) + slot, BF16),
            pltpu.VMEM((2, 16) + slot, BF16),
            pltpu.VMEM((2, 16) + slot, BF16),
            pltpu.VMEM((2, 16) + slot, BF16),
            pltpu.VMEM((N_CTX,) + slot, BF16),
            pltpu.VMEM((2, 2, 2, 16, PIECE, KW), BF16),
            pltpu.VMEM((2 * GROUP, KW), BF16),
            pltpu.VMEM((LAT, 2 * GROUP), BF16),
            pltpu.VMEM((2, KW, columns), BF16),
            pltpu.VMEM((LAT, columns), F32),
            pltpu.VMEM((8, columns), F32),
            pltpu.VMEM((8, columns), F32),
            pltpu.VMEM((9, LAT, columns), BF16),
            dma((12,)),
            dma((1,)),
            dma((2, 4)),
            dma((1,)),
            dma((2, 4)),
            dma((1,)),
            dma((2, 2)),
            dma((4,)),
            dma((13,)),
            dma((2, 2)),
            dma((2, 2)),
            dma((2,)),
            dma((2, 4)),
            dma((1,)),
            dma((2,)),
        ],
        compiler_params=pltpu.CompilerParams(
            collective_id=0, has_side_effects=True, vmem_limit_bytes=56 * 1024 * 1024
        ),
        name="attend_and_dispatch",
    )(
        positions.reshape(N_CTX, count),
        latent,
        k_rope.T,
        moe_rows,
        expert_ids.T,
        expert_weights.T,
        q_nope,
        q_rope,
        w_uk,
        w_uv,
        w_gate,
        w_up,
        w_down,
    )
    return pl.pallas_call(
        hand_over,
        out_shape=tuple(jax.ShapeDtypeStruct(r.shape, r.dtype) for r in results),
        in_specs=[vmem] * 2,
        out_specs=(vmem, vmem),
        name="hand_over",
    )(*results)


def solution(mesh):
    return jax.shard_map(
        shards,
        mesh=mesh,
        in_specs=(
            P("ctx", "ep"),
            P("ctx", "ep"),
            P("ctx", None),
            P("ctx", None),
            P(None, "ep"),
            P(None, "ep"),
            P(),
            P("ctx", "ep"),
            P("ctx", None),
            P("ctx", None),
            P("ctx", None, "ep"),
            P("ctx", None, "ep"),
            P("ctx", "ep", None),
        ),
        out_specs=(P("ctx", "ep"), P("ctx", "ep")),
        check_vma=False,
    )
```

```python
import math

import jax
import jax.numpy as jnp
from jax import lax
from jax.experimental import pallas as pl
from jax.experimental.pallas import tpu as pltpu
from jax.sharding import PartitionSpec as P

F32 = jnp.float32
BF16 = jnp.bfloat16
MESH = pl.DeviceIdType.MESH

NOPE = 128
ROPE = 64
LAT = 512
CAP = 8
N_CTX = 32
KW = LAT + 2 * ROPE
RUN = 64
PIECE = 32
GROUP = 256
BLOCK = 512
SCALE = 1.0 / math.sqrt(NOPE + ROPE)
LOG2E = math.log2(math.e)
LOW = -1e30


def dot(a, b):
    return jnp.dot(a, b, preferred_element_type=F32)


def dot_t(a, b):
    return lax.dot_general(a, b, (((1,), (1,)), ((), ())), preferred_element_type=F32)


def dot_0(a, b):
    return lax.dot_general(a, b, (((0,), (0,)), ((), ())), preferred_element_type=F32)


def iota(shape, dim):
    return lax.broadcasted_iota(jnp.int32, shape, dim)


def kernel(
    positions_h,
    latent_h,
    k_rope_h,
    rows_h,
    ids_h,
    weights_h,
    q_nope_h,
    q_rope_h,
    w_uk_h,
    w_uv_h,
    w_gate_h,
    w_up_h,
    w_down_h,
    attn_out,
    moe_out,
    positions,
    latent,
    k_rope,
    rows,
    ids,
    weights,
    q_nope,
    q_rope,
    w_uk,
    w_gate,
    w_up,
    w_down,
    index_row,
    meta,
    outgoing,
    slots,
    to_mate,
    from_mate,
    to_pair,
    kept,
    from_pair,
    returned,
    keys,
    key_group,
    value_group,
    queries,
    acc,
    row_max,
    row_sum,
    mixed,
    load_sem,
    disp_send,
    disp_recv,
    pair_send,
    pair_recv,
    core_send,
    core_recv,
    ag_send,
    ag_recv,
    back_core_send,
    back_core_recv,
    back_pair_send,
    back_pair_recv,
    back_send,
    back_recv,
):
    ctx = lax.axis_index("ctx")
    ep = lax.axis_index("ep")
    h = ctx // 16
    z = (ctx // 4) % 4
    y = ctx % 4
    lo = ep // 2
    core = ep % 2
    ep_pair = (1 - lo) * 2 + core
    ep_mate = lo * 2 + (1 - core)
    part = rows.shape[1]
    half = part // 2

    def context(step, dz, dy):
        other = h if step == 0 else 1 - h
        return other * 16 + ((z + dz) % 4) * 4 + (y + dy) % 4

    def partner_ep(step):
        return ep if step == 0 else ep_pair

    def window(step):
        return (h if step == 0 else 1 - h) * 16

    def kept_lo(step):
        return lo if step == 0 else 1 - lo

    order = [(s, dz, dy) for s in range(2) for dz in (0, 1, 3, 2) for dy in (0, 1, 3, 2)]

    loads = [
        pltpu.make_async_copy(src, dst, load_sem.at[i])
        for i, (src, dst) in enumerate(
            (
                (ids_h, ids),
                (weights_h, weights),
                (rows_h, rows),
                (k_rope_h, k_rope),
                (latent_h, latent),
                (positions_h, positions),
                (q_nope_h, q_nope),
                (q_rope_h, q_rope),
                (w_uk_h, w_uk),
                (w_gate_h.at[0], w_gate),
                (w_up_h.at[0], w_up),
                (w_down_h.at[0], w_down),
            )
        )
    ]
    for load in loads[:9]:
        load.start()

    barrier = pltpu.get_barrier_semaphore()
    for s, dz, dy in order[1:]:
        pl.semaphore_signal(
            barrier, inc=1, device_id=(context(s, dz, dy), partner_ep(s)), device_id_type=MESH
        )
    pl.semaphore_signal(barrier, inc=1, device_id=(ctx, ep_pair), device_id_type=MESH)
    pl.semaphore_signal(barrier, inc=1, device_id=(ctx, ep_mate), device_id_type=MESH)

    for load in loads[:3]:
        load.wait()
    expert = iota((128, 128), 0)
    named = jnp.zeros((128, 128), F32)
    slot_weight = jnp.zeros((128, 128), F32)
    for k in range(ids.shape[0]):
        hit = (ids[k : k + 1, :] == expert) & (expert < N_CTX)
        named = jnp.where(hit, 1.0, named)
        slot_weight = jnp.where(hit, weights[k : k + 1, :], slot_weight)
    earlier = jnp.where(expert < iota((128, 128), 1), 1.0, 0.0).astype(BF16)
    named_b = named.astype(BF16)
    rank_b = dot(named_b, earlier).astype(BF16)
    spread = jnp.where(iota((256, 128), 0) // CAP == iota((256, 128), 1), 1.0, 0.0).astype(BF16)
    picked = (dot(spread, named_b) > 0.5) & (
        dot(spread, rank_b) == (iota((256, 128), 0) % CAP).astype(F32)
    )
    pick = jnp.where(picked, 1.0, 0.0).astype(BF16)
    for c in range(4):
        lhs = pick[64 * c : 64 * (c + 1)]
        first = dot(lhs, rows[:, :half]).reshape(8, CAP, half)
        second = dot(lhs, rows[:, half:]).reshape(8, CAP, half)
        outgoing[8 * c : 8 * (c + 1)] = jnp.concatenate([first, second], axis=1).astype(BF16)

    for load in loads[3:6]:
        load.wait()
    double = jnp.where(iota((ROPE, 128), 1) % ROPE == iota((ROPE, 128), 0), 1.0, 0.0).astype(BF16)
    majors, minors = (z, y), (y, z)
    own_place = [majors[f] * 4 + minors[f] for f in range(2)]
    rotated = dot_0(k_rope[...], double)
    rotated = jnp.where(core == 0, rotated[:RUN], rotated[RUN:]).astype(BF16)
    for f in range(2):
        own_rows = pl.ds(pl.multiple_of(core * RUN + f * PIECE, PIECE), PIECE)
        keys[core, f, h, own_place[f], :, :LAT] = latent[own_rows, :]
        keys[core, f, h, own_place[f], :, LAT:] = rotated[f * PIECE : (f + 1) * PIECE]

    pl.semaphore_wait(barrier, 33)

    own = pltpu.make_async_copy(outgoing.at[ctx], slots.at[ep, ctx], disp_recv.at[0, 0])
    own.start()
    for s, dz, dy in order[1:]:
        to = context(s, dz, dy)
        pltpu.make_async_remote_copy(
            src_ref=outgoing.at[to],
            dst_ref=slots.at[ep, ctx],
            send_sem=disp_send.at[0],
            recv_sem=disp_recv.at[s, dz],
            device_id=(to, partner_ep(s)),
            device_id_type=MESH,
        ).start()

    def at_axis(f, major_to, minor_to):
        return h * 16 + (major_to * 4 + minor_to if f == 0 else minor_to * 4 + major_to)

    def send_keys(region, sent, arrived, to):
        pltpu.make_async_remote_copy(
            src_ref=region,
            dst_ref=region,
            send_sem=ag_send.at[sent],
            recv_sem=ag_recv.at[arrived],
            device_id=to,
            device_id_type=MESH,
        ).start()

    def keys_first():
        for f in range(2):
            send_keys(keys.at[core, f, h, own_place[f]], 0, 0, ((1 - h) * 16 + z * 4 + y, ep_pair))

    def keys_second(which):
        side = h if which == 0 else 1 - h
        if which == 1:
            wait_for(keys.at[core, :, side, 0], ag_recv.at[0])
        for t in (1, 3, 2):
            for f in range(2):
                to = (at_axis(f, majors[f], (minors[f] + t) % 4), ep)
                send_keys(keys.at[core, f, side, own_place[f]], 1, 1 + which, to)

    def keys_third(which):
        side = h if which == 0 else 1 - h
        wait_for(keys.at[core, :, side, pl.ds(0, 3)], ag_recv.at[1 + which])
        for t in (1, 3, 2):
            for f in range(2):
                to = (at_axis(f, (majors[f] + t) % 4, minors[f]), ep)
                region = keys.at[core, f, side, pl.ds(majors[f] * 4, 4)]
                send_keys(region, 2, 2 + 3 * which + t, to)
        for f in range(2):
            region = keys.at[core, f, side, pl.ds(majors[f] * 4, 4)]
            send_keys(region, 3, 9, (ctx, ep_mate))

    def keys_share(which, t):
        side = h if which == 0 else 1 - h
        wait_for(keys.at[core, :, side, pl.ds(0, 4)], ag_recv.at[2 + 3 * which + t])
        for f in range(2):
            at = (majors[f] - t + 4) % 4
            send_keys(keys.at[core, f, side, pl.ds(at * 4, 4)], 3, 9 + t, (ctx, ep_mate))

    def wait_for(ref, sem):
        pltpu.make_async_copy(ref, ref, sem).wait()

    keys_first()

    block = iota((N_CTX, 128), 0)
    held_0 = positions[:, 0:1] // RUN == iota((N_CTX, 128), 1)
    held_1 = positions[:, RUN : RUN + 1] // RUN == iota((N_CTX, 128), 1)
    where = jnp.sum(
        jnp.where(held_0, 2 * block, 0) + jnp.where(held_1, 2 * block + 1, 0), axis=0
    )
    index_row[...] = jnp.zeros(index_row.shape, jnp.int32)
    index_row[0:1, :] = where.reshape(1, 128)
    index_row[1:2, :] = positions[pl.ds(ctx, 1), :]
    swapped = jnp.where(positions[:, 0:1] > positions[:, RUN : RUN + 1], 1, 0)
    swapped = jnp.sum(jnp.where(block == iota((N_CTX, 128), 1), swapped, 0), axis=0)
    index_row[2:3, :] = swapped.reshape(1, 128)
    index_copy = pltpu.make_async_copy(index_row, meta, load_sem.at[0])
    index_copy.start()

    for load in loads[6:9]:
        load.wait()
    for load in loads[9:]:
        load.start()
    unit = jnp.where(iota((128, 128), 0) == iota((128, 128), 1), 1.0, 0.0).astype(BF16)

    @pl.loop(0, 8)
    def _(pair):
        at = pl.ds(pl.multiple_of(pair * 128, 128), 128)
        cols = pl.ds(pl.multiple_of(pair * 256, 256), 256)
        for run in range(2):
            of_run = slice(run * RUN, (run + 1) * RUN)
            both = q_nope[of_run, cols].astype(F32)
            first = iota(both.shape, 1) < NOPE
            apart = jnp.concatenate(
                [jnp.where(first, both, 0.0), jnp.where(first, 0.0, both)], axis=0
            ).astype(BF16)
            queries[run, :LAT, at] = dot_t(w_uk[:, cols], apart).astype(BF16)
            both = q_rope[of_run, at].astype(F32)
            first = iota(both.shape, 1) < ROPE
            apart = jnp.concatenate(
                [jnp.where(first, both, 0.0), jnp.where(first, 0.0, both)], axis=0
            ).astype(BF16)
            queries[run, LAT:, at] = dot_t(unit, apart).astype(BF16)

    index_copy.wait()
    out_weights = pltpu.make_async_copy(w_uv_h, w_uk, load_sem.at[1])
    out_weights.start()

    def chunk(step, dz, lo_part):
        return slots.at[lo_part * 2 + core, pl.ds(window(step) + ((z - dz + 4) % 4) * 4, 4)]

    def relay(step, dz):
        region = chunk(step, dz, kept_lo(step))
        wait_for(region, disp_recv.at[step, dz])
        pltpu.make_async_remote_copy(
            src_ref=region,
            dst_ref=region,
            send_sem=pair_send.at[0],
            recv_sem=pair_recv.at[step, dz],
            device_id=(ctx, ep_pair),
            device_id_type=MESH,
        ).start()
        pltpu.make_async_remote_copy(
            src_ref=region,
            dst_ref=region,
            send_sem=core_send.at[0],
            recv_sem=core_recv.at[0, step],
            device_id=(ctx, ep_mate),
            device_id_type=MESH,
        ).start()

    def relay_again(step, dz):
        region = chunk(step, dz, 1 - kept_lo(step))
        wait_for(region, pair_recv.at[step, dz])
        pltpu.make_async_remote_copy(
            src_ref=region,
            dst_ref=region,
            send_sem=core_send.at[0],
            recv_sem=core_recv.at[1, step],
            device_id=(ctx, ep_mate),
            device_id_type=MESH,
        ).start()

    def send_sums(step, dz):
        some_of = pl.ds(((z + dz) % 4) * 4, 4)
        pltpu.make_async_remote_copy(
            src_ref=to_pair.at[step, some_of],
            dst_ref=from_pair.at[step, some_of],
            send_sem=back_pair_send.at[step],
            recv_sem=back_pair_recv.at[step, dz],
            device_id=(ctx, ep_pair),
            device_id_type=MESH,
        ).start()

    def from_experts(step):
        start = window(step)
        for j in range(2):
            lo_part = kept_lo(step) if j == 0 else 1 - kept_lo(step)
            wait_for(
                slots.at[lo_part * 2 + (1 - core), pl.ds(start, 16)], core_recv.at[j, step]
            )

        def some(p, carry):
            gate, up = carry
            taken = slots[p, pl.ds(start, 16)].astype(F32)
            for i in range(2):
                x = taken[:, CAP * i : CAP * (i + 1)].reshape(128, half).astype(BF16)
                at = pl.ds(pl.multiple_of(p * part + i * half, 128), half)
                gate = gate + dot(x, w_gate[at, :])
                up = up + dot(x, w_up[at, :])
            return gate, up

        width = w_gate.shape[1]
        gate, up = lax.fori_loop(
            0, 4, some, (jnp.zeros((128, width), F32), jnp.zeros((128, width), F32))
        )
        hidden = (gate / (1.0 + jnp.exp(-gate)) * up).astype(BF16)

        def through_down(p):
            both = []
            for i in range(2):
                at = pl.ds(pl.multiple_of(p * part + i * half, 128), half)
                both.append(dot(hidden, w_down[:, at]).reshape(16, CAP, half))
            return jnp.concatenate(both, axis=1)

        for j in range(2):
            lo_part = 1 - kept_lo(step) if j == 0 else kept_lo(step)
            to_mate[step, j] = through_down(lo_part * 2 + (1 - core)).astype(BF16)
            pltpu.make_async_remote_copy(
                src_ref=to_mate.at[step, j],
                dst_ref=from_mate.at[step, j],
                send_sem=back_core_send.at[step, j],
                recv_sem=back_core_recv.at[step, j],
                device_id=(ctx, ep_mate),
                device_id_type=MESH,
            ).start()
        mine = through_down((1 - kept_lo(step)) * 2 + core)
        wait_for(from_mate.at[step, 0], back_core_recv.at[step, 0])
        to_pair[step] = (mine + from_mate[step, 0].astype(F32)).astype(BF16)
        for dz in (0, 1, 3, 2) if step == 0 else (0, 1):
            send_sums(step, dz)
        mine = through_down(kept_lo(step) * 2 + core)
        wait_for(from_mate.at[step, 1], back_core_recv.at[step, 1])
        kept[step] = (mine + from_mate[step, 1].astype(F32)).astype(BF16)

    def send_back(step, dz):
        start = ((z + dz) % 4) * 4
        some_of = pl.ds(start, 4)
        wait_for(from_pair.at[step, some_of], back_pair_recv.at[step, dz])
        base = window(step) + start
        outgoing[pl.ds(base, 4)] = (
            kept[step, some_of].astype(F32) + from_pair[step, some_of].astype(F32)
        ).astype(BF16)
        for dy in (0, 1, 3, 2):
            to = base + (y + dy) % 4

            def send(to=to):
                pltpu.make_async_remote_copy(
                    src_ref=outgoing.at[to],
                    dst_ref=returned.at[ctx],
                    send_sem=back_send.at[0],
                    recv_sem=back_recv.at[step],
                    device_id=(to, partner_ep(step)),
                    device_id_type=MESH,
                ).start()

            if step == 0 and dy == 0:
                pl.when(dz != 0)(send)

                @pl.when(dz == 0)
                def _():
                    pltpu.make_async_copy(
                        outgoing.at[ctx], returned.at[ctx], back_recv.at[0]
                    ).start()

            else:
                send()

    run_0 = meta[1, 0] // RUN
    run_1 = meta[1, RUN] // RUN
    run_late = jnp.maximum(run_0, run_1)
    run_early = jnp.minimum(run_0, run_1)
    late_half = jnp.where(run_1 > run_0, 1, 0)
    late_steps = run_late // 4 + 1
    columns = queries.shape[2]

    def take_values(count):
        for t in range(count // 128):
            at = slice(t * 128, (t + 1) * 128)
            value_group[:, at] = key_group[at, :LAT].T

    def take_early(t):
        for f in range(2):
            row = (majors[f] - t + 4) % 4
            for n in range(8):
                side, a = n // 4, n % 4
                c = side * 16 + (row * 4 + a if f == 0 else a * 4 + row)
                to = (f * 8 + n) * PIECE
                key_group[to : to + PIECE, :] = jnp.where(
                    meta[2, c] == 1, keys[1, f, side, row * 4 + a], keys[0, f, side, row * 4 + a]
                )
        take_values(2 * GROUP)

    def take_keys(group, count):
        for t in range(count // RUN):
            at = jnp.clip(meta[0, group * 4 + t], 0, 2 * N_CTX - 1)
            of, c = at % 2, at // 2
            z_at, y_at = (c // 4) % 4, c % 4
            first, second = t * RUN, t * RUN + PIECE
            key_group[first:second, :] = keys[of, 0, c // 16, z_at * 4 + y_at]
            key_group[second : second + PIECE, :] = keys[of, 1, c // 16, y_at * 4 + z_at]
        take_values(count)

    def attend(i, wide):
        if wide:
            count, q_half = 2 * GROUP, late_half
            take_early(i)
        else:
            is_late = i < late_steps
            count = GROUP
            group = jnp.where(is_late, i, i - late_steps)
            q_half = jnp.where(is_late, late_half, 1 - late_half)
            q_run = jnp.where(is_late, run_late, run_early)
            turn = i == late_steps
            take_keys(group, count)

        def scores_of(b):
            scores = dot(
                key_group[:count, :], queries[q_half, :, b * BLOCK : (b + 1) * BLOCK]
            )
            if not wide:
                key_pos = group * GROUP + iota(scores.shape, 0)
                query_pos = q_run * RUN + iota(scores.shape, 1) % RUN
                scores = jnp.where(key_pos <= query_pos, scores, LOW)
            return scores

        following = scores_of(0)
        for b in range(columns // BLOCK):
            at = slice(b * BLOCK, (b + 1) * BLOCK)
            scores = following
            if (b + 1) * BLOCK < columns:
                following = scores_of(b + 1)
            old_max = row_max[:, at]
            if not wide:
                old_max = jnp.where(turn, LOW, old_max)
            new_max = jnp.maximum(old_max, jnp.max(scores, axis=0, keepdims=True))
            fade = jnp.exp2((old_max - new_max) * (SCALE * LOG2E))
            probs = jnp.exp2((scores - new_max[:1]) * (SCALE * LOG2E))
            new_sum = row_sum[:, at] * fade + jnp.sum(
                probs.reshape(count // 8, 8, BLOCK), axis=0
            )
            new_acc = acc[:, at] * fade[:1] + dot(value_group[:, :count], probs.astype(BF16))
            row_max[:, at] = new_max
            row_sum[:, at] = new_sum
            acc[:, at] = new_acc
            if not wide:
                whole = jnp.sum(new_sum, axis=0, keepdims=True)
                mixed[i - 8, :, at] = (new_acc * (1.0 / whole)).astype(BF16)

    row_max[...] = jnp.full(row_max.shape, LOW, F32)
    row_sum[...] = jnp.zeros(row_sum.shape, F32)
    acc[...] = jnp.zeros(acc.shape, F32)

    def gray(i):
        return jnp.where(i < 2, i, 5 - i)

    def attend_early(t):
        wait_for(keys.at[1 - core, :, :, pl.ds(0, 4)], ag_recv.at[9 + t])
        attend(t, True)

    relay(0, 0)
    keys_second(0)
    relay(0, 1)
    keys_second(1)
    relay(0, 3)
    relay(0, 2)
    relay(1, 0)
    keys_third(0)
    relay(1, 1)
    keys_third(1)
    relay(1, 3)
    relay(1, 2)
    relay_again(0, 0)
    relay_again(0, 1)
    relay_again(0, 3)
    relay_again(0, 2)
    for load in loads[9:]:
        load.wait()
    wait_for(outgoing.at[pl.ds(0, 31)], disp_send.at[0])
    from_experts(0)
    keys_share(0, 1)
    relay_again(1, 0)
    keys_share(0, 3)
    relay_again(1, 1)
    keys_share(0, 2)
    relay_again(1, 3)
    relay_again(1, 2)
    from_experts(1)
    keys_share(1, 1)
    attend_early(0)
    send_back(0, 0)
    send_back(0, 1)
    send_sums(1, 3)
    keys_share(1, 3)
    attend_early(1)
    send_back(0, 3)
    send_sums(1, 2)
    send_back(0, 2)
    keys_share(1, 2)
    attend_early(3)
    attend_early(2)
    send_back(1, 0)

    @pl.loop(0, 3)
    def _(i):
        attend(8 + 2 * i, False)
        attend(9 + 2 * i, False)
        send_back(1, gray(1 + i))

    @pl.loop(14, 17)
    def _(i):
        attend(i, False)

    out_weights.wait()
    late_at = jnp.clip(late_steps - 9, 0, 7)

    @pl.loop(0, 8)
    def _(pair):
        at = pl.ds(pl.multiple_of(pair * 128, 128), 128)
        for run in range(2):
            place = jnp.where(late_half == run, late_at, 8)
            cols = pl.ds(pl.multiple_of(pair * 256, 256), 256)
            both = dot_0(mixed[place, :, at], w_uk[:, cols])
            for i in range(2):
                to = pl.ds(pl.multiple_of(pair * 256 + i * 128, 128), 128)
                attn_out[run * RUN : (run + 1) * RUN, to] = both[
                    i * RUN : (i + 1) * RUN, i * 128 : (i + 1) * 128
                ].astype(BF16)

    wide = (128, N_CTX * 2 * CAP)
    column = iota(wide, 1)
    spread_2 = jnp.where(column // (2 * CAP) == iota(wide, 0), 1.0, 0.0).astype(BF16)
    weight_hi = slot_weight.astype(BF16)
    weight_lo = (slot_weight - weight_hi.astype(F32)).astype(BF16)
    here = (dot_0(named_b, spread_2) > 0.5) & (
        dot_0(rank_b, spread_2) == (column % CAP).astype(F32)
    )
    parts = [dot_0(w, spread_2) for w in (weight_hi, weight_lo)]
    wait_for(returned.at[pl.ds(0, 16)], back_recv.at[0])
    wait_for(returned.at[pl.ds(0, 16)], back_recv.at[1])
    for i in range(2):
        mine = here & ((column // CAP) % 2 == i)
        total = jnp.zeros((128, half), F32)
        for w in parts:
            factor = jnp.where(mine, w, 0.0).astype(BF16)
            total = total + dot(factor, returned[...].reshape(N_CTX * 2 * CAP, half))
        moe_out[:, i * half : (i + 1) * half] = total.astype(BF16)

    wait_for(slots.at[0], pair_send.at[0])
    wait_for(slots.at[pl.ds(0, 2)], core_send.at[0])
    wait_for(keys.at[0, :, 0, 0], ag_send.at[0])
    wait_for(keys.at[0, 0, 0, pl.ds(0, 12)], ag_send.at[1])
    wait_for(keys.at[0, :, :, pl.ds(0, 12)], ag_send.at[2])
    wait_for(keys.at[0], ag_send.at[3])
    for step in range(2):
        for j in range(2):
            wait_for(to_mate.at[step, j], back_core_send.at[step, j])
        wait_for(to_pair.at[step], back_pair_send.at[step])
    wait_for(outgoing.at[pl.ds(0, 31)], back_send.at[0])


def hand_over(attn, moe, attn_out, moe_out):
    attn_out[...] = attn[...]
    moe_out[...] = moe[...]


def shards(
    q_nope,
    q_rope,
    latent,
    k_rope,
    w_uk,
    w_uv,
    positions,
    moe_rows,
    expert_ids,
    expert_weights,
    w_gate,
    w_up,
    w_down,
):
    count, part = moe_rows.shape
    half = part // 2
    vmem = pl.BlockSpec(memory_space=pltpu.VMEM)
    anywhere = pl.BlockSpec(memory_space=pl.ANY)
    dma = pltpu.SemaphoreType.DMA
    columns = q_nope.shape[1] // NOPE * RUN
    slot = (2 * CAP, half)
    results = pl.pallas_call(
        kernel,
        out_shape=(
            jax.ShapeDtypeStruct(q_nope.shape, BF16),
            jax.ShapeDtypeStruct(moe_rows.shape, BF16),
        ),
        in_specs=[anywhere] * 13,
        out_specs=(vmem, vmem),
        scratch_shapes=[
            pltpu.VMEM((N_CTX, count), jnp.int32),
            pltpu.VMEM(latent.shape, BF16),
            pltpu.VMEM(k_rope.shape[::-1], BF16),
            pltpu.VMEM(moe_rows.shape, BF16),
            pltpu.VMEM(expert_ids.shape[::-1], jnp.int32),
            pltpu.VMEM(expert_weights.shape[::-1], F32),
            pltpu.VMEM(q_nope.shape, BF16),
            pltpu.VMEM(q_rope.shape, BF16),
            pltpu.VMEM(w_uk.shape, BF16),
            pltpu.VMEM(w_gate.shape[1:], BF16),
            pltpu.VMEM(w_up.shape[1:], BF16),
            pltpu.VMEM(w_down.shape[1:], BF16),
            pltpu.VMEM((8, 128), jnp.int32),
            pltpu.SMEM((8, 128), jnp.int32),
            pltpu.VMEM((N_CTX,) + slot, BF16),
            pltpu.VMEM((4, N_CTX) + slot, BF16),
            pltpu.VMEM((2, 2, 16) + slot, BF16),
            pltpu.VMEM((2, 2, 16) + slot, BF16),
            pltpu.VMEM((2, 16) + slot, BF16),
            pltpu.VMEM((2, 16) + slot, BF16),
            pltpu.VMEM((2, 16) + slot, BF16),
            pltpu.VMEM((N_CTX,) + slot, BF16),
            pltpu.VMEM((2, 2, 2, 16, PIECE, KW), BF16),
            pltpu.VMEM((2 * GROUP, KW), BF16),
            pltpu.VMEM((LAT, 2 * GROUP), BF16),
            pltpu.VMEM((2, KW, columns), BF16),
            pltpu.VMEM((LAT, columns), F32),
            pltpu.VMEM((8, columns), F32),
            pltpu.VMEM((8, columns), F32),
            pltpu.VMEM((9, LAT, columns), BF16),
            dma((12,)),
            dma((1,)),
            dma((2, 4)),
            dma((1,)),
            dma((2, 4)),
            dma((1,)),
            dma((2, 2)),
            dma((4,)),
            dma((13,)),
            dma((2, 2)),
            dma((2, 2)),
            dma((2,)),
            dma((2, 4)),
            dma((1,)),
            dma((2,)),
        ],
        compiler_params=pltpu.CompilerParams(
            collective_id=0, has_side_effects=True, vmem_limit_bytes=56 * 1024 * 1024
        ),
        name="attend_and_dispatch",
    )(
        positions.reshape(N_CTX, count),
        latent,
        k_rope.T,
        moe_rows,
        expert_ids.T,
        expert_weights.T,
        q_nope,
        q_rope,
        w_uk,
        w_uv,
        w_gate,
        w_up,
        w_down,
    )
    return pl.pallas_call(
        hand_over,
        out_shape=tuple(jax.ShapeDtypeStruct(r.shape, r.dtype) for r in results),
        in_specs=[vmem] * 2,
        out_specs=(vmem, vmem),
        name="hand_over",
    )(*results)


def solution(mesh):
    return jax.shard_map(
        shards,
        mesh=mesh,
        in_specs=(
            P("ctx", "ep"),
            P("ctx", "ep"),
            P("ctx", None),
            P("ctx", None),
            P(None, "ep"),
            P(None, "ep"),
            P(),
            P("ctx", "ep"),
            P("ctx", None),
            P("ctx", None),
            P("ctx", None, "ep"),
            P("ctx", None, "ep"),
            P("ctx", "ep", None),
        ),
        out_specs=(P("ctx", "ep"), P("ctx", "ep")),
        check_vma=False,
    )
```
